512 devices in a mesh: gx: 128 (over x, z, y_hi), gy: 4 (over y_lo, core).
Axes of the slice: x: 4, y: 8 (y_hi: 4, y_lo: 2; y = y_hi * 2 + y_lo), z: 8, core: 2. Of those that a mesh axis runs over, the one named last changes fastest.
Arguments:
- wave_sq: float32 [1024, 128, 512], P('gx', 'gy'), may hold values from 0.2 to 2
- absorb: float32 [1024, 128, 512], P('gx', 'gy'), may hold values from 0.05 to 0.5
Outputs:
- level_one: float32 [2, 3, 3, 3, 512, 64, 256], P(None, None, None, None, 'gx', 'gy')
- level_two: float32 [2, 3, 3, 3, 256, 32, 128], P(None, None, None, None, 'gx', 'gy')
- level_three: float32 [2, 3, 3, 3, 128, 16, 64], P(None, None, None, None, 'gx')
The draws below stay inside these ranges and needn't reach their ends.
All inputs are finite; a program needn't handle non-finite values.
Results may differ from the reference program's by a relative error of at most 0.0001.
Values sent between devices are 32-bit elements; how exact they have to be, the bound alone decides.
A program may use at most 64 MiB of HBM per device.

```python
import math
import jax
import jax.numpy as jnp
from jax import lax

NZ = 512
NX = 1024
NY = 128


def block_scale(own_key, shape, shards, least, top_value):
    factor_of, own = 1.0, jax.random.fold_in(own_key, 6)
    for dim, parts in shards:
        steps = jnp.exp(jax.random.uniform(jax.random.fold_in(own, dim), (parts,), jnp.float32, least / len(shards), top_value / len(shards)))
        factor_of = factor_of * jnp.repeat(steps, shape[dim] // parts).reshape([-1 if axis == dim else 1 for axis in range(len(shape))])
    return factor_of


def setup_inputs(seed: int = 0) -> dict:
    key_of = jax.random.split(jax.random.key(seed), 3)
    wave_sq = jnp.clip(jnp.exp(math.log(2.0) - 2.3025851 * jax.random.uniform(key_of[0], (NX, NY, NZ), jnp.float32) ** block_scale(key_of[0], (NX, NY, NZ), ((0, 128), (1, 4)), -0.2, 0.2)), 0.2, 2.0)
    absorb = jnp.clip(jnp.exp(math.log(0.5) - 2.3025851 * jax.random.uniform(key_of[1], (NX, NY, NZ), jnp.float32) ** block_scale(key_of[1], (NX, NY, NZ), ((0, 128), (1, 4)), -0.2, 0.2)), 0.05, 0.5)
    return dict(wave_sq=wave_sq, absorb=absorb)


RESTRICT = (0.25, 0.5, 0.25)


def spread_weight(distance):
    if distance == 0:
        return 1.0
    if abs(distance) == 1:
        return 0.5
    return 0.0


def pad_front(array, axis):
    widths = [(0, 0)] * array.ndim
    widths[axis] = (1, 0)
    return jnp.pad(array, widths)


def coarsen(stencil, offset_axis, cell_axis, anchor, extent):
    length = stencil.shape[cell_axis]
    halves = (length - 1) // 2
    pieces = [lax.slice_in_dim(stencil, first_cell, first_cell + 2 * halves - 1, 2, cell_axis) for first_cell in (0, 1, 2)]
    offsets_in = stencil.shape[offset_axis]
    fine_offsets = (0,) if offsets_in == 1 else (-1, 0, 1)
    mask_shape = list(pieces[0].shape)
    mask_shape[offset_axis] = 1
    position = anchor + lax.broadcasted_iota(jnp.int32, tuple(mask_shape), cell_axis)
    blocks = []
    for coarse_off in (-1, 0, 1):
        summed = jnp.zeros(tuple(mask_shape), stencil.dtype)
        for fine_step in (-1, 0, 1):
            for fine_off in fine_offsets:
                factor = RESTRICT[fine_step + 1] * spread_weight(fine_step + fine_off - 2 * coarse_off)
                if factor != 0.0:
                    offset_slot = 0 if offsets_in == 1 else fine_off + 1
                    summed = summed + factor * lax.slice_in_dim(pieces[fine_step + 1], offset_slot, offset_slot + 1, 1, offset_axis)
        inside = (position + coarse_off >= 0) & (position + coarse_off < extent)
        blocks.append(jnp.where(inside, summed, 0.0))
    return jnp.concatenate(blocks, axis=offset_axis)


def line_tables(cells):
    places = jnp.arange(cells, dtype=jnp.int32)
    lower = jnp.where(places >= 1, -1.0, 0.0).astype(jnp.float32)
    upper = jnp.where(places <= cells - 2, -1.0, 0.0).astype(jnp.float32)
    lap_line = jnp.stack([lower, jnp.full((cells,), 2.0, jnp.float32), upper])
    one_line = jnp.ones((1, cells), jnp.float32)
    tables = []
    for coarse_level in range(3):
        lap_line = coarsen(pad_front(lap_line, 1), 0, 1, 0, lap_line.shape[1] // 2)
        one_line = coarsen(pad_front(one_line, 1), 0, 1, 0, one_line.shape[1] // 2)
        tables.append((lap_line, one_line))
    return tables


def along_x(line):
    return line[:, None, None, :, None, None]


def along_y(line):
    return line[None, :, None, None, :, None]


def along_z(line):
    return line[None, None, :, None, None, :]


def assemble(stencil, lap_x, one_x, lap_y, one_y, lap_z, one_z):
    grid = along_x(lap_x) * along_y(one_y) * along_z(one_z)
    grid = grid + along_x(one_x) * along_y(lap_y) * along_z(one_z)
    grid = grid + along_x(one_x) * along_y(one_y) * along_z(lap_z)
    return jnp.stack([grid - stencil[0], -stencil[1]])


def reference(wave_sq, absorb):
    stencil = jnp.stack([wave_sq + 0.5 * absorb, absorb - 0.5 * wave_sq])[:, None, None, None]
    tables_x = line_tables(wave_sq.shape[0])
    tables_y = line_tables(wave_sq.shape[1])
    tables_z = line_tables(wave_sq.shape[2])
    results = []
    for coarse_level in range(3):
        for cell_axis in (4, 5, 6):
            cells = stencil.shape[cell_axis]
            stencil = coarsen(pad_front(stencil, cell_axis), cell_axis - 3, cell_axis, 0, cells // 2)
        lap_x, one_x = tables_x[coarse_level]
        lap_y, one_y = tables_y[coarse_level]
        lap_z, one_z = tables_z[coarse_level]
        results.append(assemble(stencil, lap_x, one_x, lap_y, one_y, lap_z, one_z))
    return (results[0], results[1], results[2])
```

```python
import functools

import jax
import jax.numpy as jnp
import ml_dtypes
import numpy as np
from jax import lax
from jax.experimental import pallas as pl
from jax.experimental.pallas import tpu as pltpu
from jax.sharding import PartitionSpec as P

MESH = pl.DeviceIdType.MESH
BF16 = jnp.bfloat16
F32 = jnp.float32
FIRST, MIDDLE, LAST = 0, 1, 2


def hat(distance, width):
    return np.maximum(0.0, 1.0 - np.abs(distance) / width)


def line_weights(cells, level, place):
    width = 2**level
    coarse = cells // width
    fine = np.arange(cells)[None, :]
    node = width * np.arange(coarse)[:, None]
    table = np.stack([hat(fine - node, width) * hat(fine - node - a * width, width) for a in (-1, 0, 1)])
    table /= width
    if place == LAST:
        table[2, -1] = 0.0
    return table


def tail_weights(cells, level, place):
    width = 2**level
    distance = np.arange(cells) - cells
    table = np.stack([hat(distance, width) * hat(distance + width, width), hat(distance, width) ** 2]) / width
    return table * (place != LAST)


def grid_tables(cells):
    lap = np.zeros((cells, 3))
    lap[:] = (-1.0, 2.0, -1.0)
    lap[0, 0] = lap[-1, 2] = 0.0
    one = np.zeros((cells, 3))
    one[:, 1] = 1.0

    def coarsen(band):
        coarse = band.shape[0] // 2
        out = np.zeros((coarse, 3))
        for row in range(coarse):
            for a in (-1, 0, 1):
                if not 0 <= row + a < coarse:
                    continue
                for step, weight in ((-1, 0.25), (0, 0.5), (1, 0.25)):
                    fine = 2 * row + step
                    if fine < 0:
                        continue
                    for b in (-1, 0, 1):
                        distance = abs(fine + b - 2 * (row + a))
                        spread = 1.0 if distance == 0 else 0.5 if distance == 1 else 0.0
                        out[row, a + 1] += weight * spread * band[fine, b + 1]
        return out

    tables = []
    for _ in range(3):
        lap, one = coarsen(lap), coarsen(one)
        tables.append((lap.T, one.T))
    return tables


def two_terms(table):
    high = table.astype(ml_dtypes.bfloat16).astype(np.float64)
    return high, table - high


def row_features(lap, one):
    (lh, ll), (oh, ol) = two_terms(lap), two_terms(one)
    columns = [lh, lh, ll, ll, oh, oh, ol, ol]
    return np.stack(columns + [np.zeros_like(lh)] * 8, axis=1)


def column_features(lap, one):
    (lh, ll), (oh, ol) = two_terms(lap), two_terms(one)
    rows = [oh, ol, oh, ol, lh, ll, lh, ll]
    return np.stack(rows + [np.zeros_like(lh)] * 8, axis=0)


def place_slice(table, place, cells):
    whole = table.shape[1]
    start = {FIRST: 0, MIDDLE: cells, LAST: whole - cells}[place]
    return table[:, start : start + cells]


def grid_rows(grid_x, grid_y, place_x, place_y, cells_x, cells_y):
    lap_x, one_x = (place_slice(t, place_x, cells_x)[:, None, :, None] for t in grid_x)
    lap_y, one_y = (place_slice(t, place_y, cells_y)[None, :, None, :] for t in grid_y)
    lap = (lap_x * one_y + one_x * lap_y).reshape(-1)
    one = (one_x * one_y).reshape(-1)
    return row_features(lap, one)


def padded(rows, count, width=None):
    out = np.zeros((count, rows.shape[1] if width is None else width))
    out[: rows.shape[0], : rows.shape[1]] = rows
    return out


def pair(left, right):
    both = np.einsum("aJi,bKj->abJKij", left, right)
    return both.reshape(-1, left.shape[2] * right.shape[2])


def xy_tables(nx, ny, sx, sy):
    grid_x, grid_y = grid_tables(nx * sx), grid_tables(ny * sy)
    first, later = [], []
    for px in (FIRST, MIDDLE, LAST):
        for py in (FIRST, MIDDLE, LAST):
            wx = [line_weights(nx, k, px) for k in (1, 2, 3)]
            wy = [line_weights(ny, k, py) for k in (1, 2, 3)]
            tx = [tail_weights(nx, k, px)[:, None, :] for k in (1, 2, 3)]
            ty = [tail_weights(ny, k, py)[:, None, :] for k in (1, 2, 3)]

            own = pair(wx[0], wy[0])
            head_x = np.zeros((3, nx // 2, 1))
            head_x[0:2, 0, 0] = 0.125 * (px != FIRST)
            head_y = np.zeros((3, ny // 2, 1))
            head_y[0:2, 0, 0] = 0.125 * (py != FIRST)
            halo = np.concatenate([pair(head_x, wy[0]), pair(wx[0], head_y), pair(head_x, head_y)], axis=1)
            halo = padded(halo, halo.shape[0], HALO)
            grid = grid_rows(grid_x[0], grid_y[0], px, py, nx // 2, ny // 2)
            first.append(padded(np.concatenate([own, halo, halo, grid], axis=1), own.shape[0], nx * ny + 128))

            m, n = nx // 4, ny // 4
            own = pair(wx[1], wy[1])
            send = [pair(tx[1], wy[1][1:]), pair(wx[1][1:], ty[1]), pair(tx[1], ty[1])]
            rows2 = padded(np.concatenate([own, *send]), 192)
            take = np.zeros((3, 3, m, n, HALO))
            for a in range(2):
                for j in range(n):
                    take[a, 1, 0, j, a * 2 * n + j] = 1.0
                    take[a, 2, 0, j, a * 2 * n + n + j] = 1.0
                    if j + 1 < n:
                        take[a, 0, 0, j + 1, a * 2 * n + n + j] = 1.0
                for i in range(m):
                    own_e, own_f = 4 * n + a * m + i, 4 * n + (2 + a) * m + i
                    take[1, a, i, 0, own_e] = 1.0
                    take[2, a, i, 0, own_f] = 1.0
                    if i + 1 < m:
                        take[0, a, i + 1, 0, own_f] = 1.0
                for b in range(2):
                    take[a, b, 0, 0, 4 * n + 4 * m + 2 * a + b] = 1.0
            take = take.reshape(-1, HALO)
            grid = grid_rows(grid_x[1], grid_y[1], px, py, m, n)
            take2 = np.concatenate([take, take, grid], axis=1)

            n = ny // 8
            own = padded(pair(wx[2], wy[2][1:]), 32)
            send = [pair(tx[2], wy[2][1:]), pair(wx[2][1:], ty[2]), pair(tx[2], ty[2])]
            rows3 = padded(np.concatenate([own, *send]), 64)
            take = np.zeros((3, 2, n, 32))
            for a in range(2):
                for e in range(2):
                    for j in range(n):
                        take[a, e, j, (a * 2 + e) * n + j] = 1.0
                take[1 + a, 0, 0, 4 * n + 2 * a + 1] = 1.0
                take[a, 0, 0, 4 * n + 4 + 2 * a + 1] = 1.0
            take = take.reshape(-1, 32)
            grid = grid_rows(grid_x[2], grid_y[2], px, py, 1, n).reshape(3, 3, n, 16)[:, 1:].reshape(-1, 16)
            take3 = np.concatenate([take, take, grid], axis=1)

            table = np.zeros((320, nx * ny + 128))
            high, low = two_terms(rows3)
            table[:, : nx * ny] = np.concatenate([rows2, high, low])
            table[: take2.shape[0], nx * ny : nx * ny + take2.shape[1]] = take2
            table[192 : 192 + take3.shape[0], nx * ny : nx * ny + take3.shape[1]] = take3
            later.append(table)
    return np.stack(first), np.stack(later)


def z_tables(nz):
    grid = grid_tables(nz)
    half = nz // 2
    blocks = []
    one = line_weights(nz, 1, LAST)
    one[0, 0] = 0.0
    for a in range(3):
        blocks.append(np.concatenate([one[a].T, column_features(grid[0][0][a], grid[0][1][a])]))
    for k in (2, 3):
        table = line_weights(nz, k, LAST)
        columns = [
            np.concatenate([table[a].T, column_features(grid[k - 1][0][a], grid[k - 1][1][a])]) for a in (1, 2)
        ]
        block = np.concatenate(columns, axis=1)
        blocks.append(padded(block, nz + 16, half))
    return np.stack(blocks)


def gather_table(parts, n):
    table = np.zeros((3, 3, parts * n, parts, 3, 2, n))
    for a in range(3):
        for g in range(parts):
            for j in range(n):
                row = g * n + j
                table[a, 1, row, g, a, 0, j] = 1.0
                table[a, 2, row, g, a, 1, j] = 1.0
                if row + 1 < parts * n:
                    table[a, 0, row + 1, g, a, 1, j] = 1.0
    table = table.reshape(9 * parts * n, -1)
    return np.concatenate([table, table], axis=1)


HALO = 48


def split(value):
    high = value.astype(BF16)
    return high, (value - high.astype(F32)).astype(BF16)


def dot(left, right):
    return jnp.dot(left, right, preferred_element_type=F32)


def exact_dot(left, value):
    high, low = split(value)
    return dot(left, high) + dot(left, low)


def halo_kernel(
    sx, sy,
    w_hbm, a_hbm, first_hbm, later_hbm, z_hbm, gather_hbm,
    one_ref, two_ref, three_ref,
    w_ref, a_ref, first_ref, later_ref, z_ref, gather_ref,
    mass, plane, row_send, row_got, corner_send, corner_got,
    x2_send, x2_got, x3_send, x3_got, blocks, t2, t3, k2, k3, raw,
    load_sem, send_sem, got_sem,
):
    ix, iy = lax.axis_index("gx"), lax.axis_index("gy")
    nx, ny, nz = w_hbm.shape
    cells = nx * ny
    next_x, last_x = lax.rem(ix + 1, sx), lax.rem(ix + sx - 1, sx)
    next_y, last_y = lax.rem(iy + 1, sy), lax.rem(iy + sy - 1, sy)
    peers = [lax.rem(iy + step, sy) for step in range(1, sy)]

    place_x = jnp.where(ix == 0, FIRST, jnp.where(ix == sx - 1, LAST, MIDDLE))
    place_y = jnp.where(iy == 0, FIRST, jnp.where(iy == sy - 1, LAST, MIDDLE))
    place = place_x * 3 + place_y
    loads = [
        pltpu.make_async_copy(src, dst, load_sem.at[i])
        for i, (src, dst) in enumerate(
            (
                (w_hbm, w_ref),
                (a_hbm, a_ref),
                (later_hbm.at[place], later_ref),
                (z_hbm.at[pl.ds(3, 2)], z_ref.at[pl.ds(3, 2)]),
                (z_hbm.at[pl.ds(0, 3)], z_ref.at[pl.ds(0, 3)]),
                (first_hbm.at[place], first_ref),
                (gather_hbm, gather_ref),
            )
        )
    ]
    for load in loads:
        load.start()

    barrier = pltpu.get_barrier_semaphore()
    sources = [(last_x, iy), (last_x, last_y)] + [(ix, p) for p in peers]
    for device in sources:
        pl.semaphore_signal(barrier, inc=1, device_id=device, device_id_type=MESH)
    pl.semaphore_wait(barrier, len(sources))

    def send(slot, src, dst, device):
        copy = pltpu.make_async_remote_copy(
            src_ref=src, dst_ref=dst, send_sem=send_sem.at[slot], recv_sem=got_sem.at[slot],
            device_id=device, device_id_type=MESH,
        )
        copy.start()
        return copy

    plane_w = send(0, w_hbm.at[nx - 1], plane.at[0], (next_x, iy))
    plane_a = send(1, a_hbm.at[nx - 1], plane.at[1], (next_x, iy))

    loads[0].wait()
    loads[1].wait()
    for x in range(nx):
        w, a = w_ref[x], a_ref[x]
        for part, value in enumerate((-(w + 0.5 * a), 0.5 * w - a)):
            high, low = split(value)
            mass[part, 0, x * ny : (x + 1) * ny] = high
            mass[part, 1, x * ny : (x + 1) * ny] = low
            for c in range(nz // 128):
                raw[part, c, x : x + 1] = value[ny - 1 : ny, c * 128 : (c + 1) * 128]
    loads[2].wait()
    loads[3].wait()

    for part in range(2):
        table = later_ref[:, 0:cells]
        rows = dot(table, mass[part, 0]) + dot(table, mass[part, 1])
        high, low = split(rows[0:192])
        two = dot(high, z_ref[3, 0:nz]) + dot(low, z_ref[3, 0:nz])
        high, low = split(rows[192:256] + rows[256:320])
        three = dot(high, z_ref[4, 0:nz, 0:128]) + dot(low, z_ref[4, 0:nz, 0:128])
        t2[part] = two[0:144]
        t3[part] = three[0:32]
        x3_send[part * 16 : part * 16 + 16] = three[32:48]
        x2_send[part * 32 : part * 32 + 32] = two[144:176]
        for e in range(2):
            row_send[64 + e * 16 + part * 8 : 64 + e * 16 + part * 8 + 8] = two[176:184, e * 128 : e * 128 + 128]
            corner_send[8 + e * 8 + part * 4 : 8 + e * 8 + part * 4 + 4] = two[184:188, e * 128 : e * 128 + 128]
        row_send[96 + part * 4 : 96 + part * 4 + 4] = three[48:52]
        corner_send[24 + part * 4 : 24 + part * 4 + 4] = three[52:56]
        for c in range(nz // 128):
            row_send[part * 32 + c * 8 : part * 32 + c * 8 + 8] = raw[part, c]
            corner_send[part * 4 + c : part * 4 + c + 1] = raw[part, c, nx - 1 : nx]

    x3 = send(2, x3_send, x3_got, (next_x, iy))
    x2 = send(3, x2_send, x2_got, (next_x, iy))
    row = send(4, row_send, row_got, (ix, next_y))
    corner = send(5, corner_send, corner_got, (next_x, next_y))

    loads[4].wait()
    loads[5].wait()

    def own_level_one(i, carry):
        part, a = i // 3, lax.rem(i, 3)
        table = z_ref[a]
        z = dot(mass[part, 0], table[0:nz]) + dot(mass[part, 1], table[0:nz])
        high, low = split(z)
        grid = jnp.where(part == 0, table[nz : nz + 16], jnp.zeros((16, nz // 2), BF16))
        rest = jnp.concatenate([jnp.zeros((2 * HALO, nz // 2), BF16), grid, jnp.zeros((16, nz // 2), BF16)], axis=0)
        for ax in range(3):
            rows = first_ref[ax * 192 : ax * 192 + 192]
            out = dot(rows[:, 0:cells], high) + dot(rows[:, 0:cells], low) + dot(rows[:, cells:], rest)
            one_ref[part, ax, :, a] = out.reshape(3, nx // 2, ny // 2, nz // 2)
        return carry

    lax.fori_loop(0, 6, own_level_one, 0)

    row.wait_recv()
    corner.wait_recv()
    x3.wait_recv()
    for part in range(2):
        k3[part, 0:16] = x3_got[part * 16 : part * 16 + 16]
        k3[part, 16:20] = row_got[96 + part * 4 : 96 + part * 4 + 4]
        k3[part, 20:24] = corner_got[24 + part * 4 : 24 + part * 4 + 4]
        k3[part, 24:32] = jnp.zeros((8, 128), F32)
        high, low = split(k3[part])
        grid = z_ref[4, nz : nz + 16, 0:128]
        if part == 1:
            grid = jnp.zeros_like(grid)
        rest = jnp.concatenate([high, low, grid, jnp.zeros((48, 128), BF16)], axis=0)
        own = t3[part] + dot(later_ref[192:224, cells:], rest)
        blocks[iy, part * 24 : part * 24 + 24] = own[0:24]
    gathers = [send(6 + i, blocks.at[iy], blocks.at[iy], (ix, p)) for i, p in enumerate(peers)]

    plane_w.wait_recv()
    plane_a.wait_recv()
    for part in range(2):
        w, a = plane[0], plane[1]
        value = -(w + 0.5 * a) if part == 0 else 0.5 * w - a
        rows = jnp.concatenate([row_got[part * 32 + c * 8 : part * 32 + c * 8 + 8] for c in range(nz // 128)], axis=1)
        edge = jnp.concatenate([corner_got[part * 4 + c : part * 4 + c + 1] for c in range(nz // 128)], axis=1)
        high, low = split(jnp.concatenate([value, rows, edge, jnp.zeros((7, nz), F32)], axis=0))
        for a in range(3):
            z = dot(high, z_ref[a, 0:nz]) + dot(low, z_ref[a, 0:nz])
            zh, zl = split(z)
            rest = jnp.concatenate([zh, zl, jnp.zeros((32, nz // 2), BF16)], axis=0)
            table = first_ref[:, cells:].reshape(3, 3, nx // 2, ny // 2, 128)
            add = dot(table[0:2, :, 0].reshape(-1, 128), rest)
            one_ref[part, 0:2, :, a, 0] += add.reshape(2, 3, ny // 2, nz // 2)
            add = dot(table[2, 0:2].reshape(-1, 128), rest).reshape(2, nx // 2, ny // 2, nz // 2)
            one_ref[part, 2, 0:2, a, :, 0:8] += add[:, :, 0:8]
            add = dot(table[0:2, 0:2, 1:].reshape(-1, 128), rest).reshape(2, 2, nx // 2 - 1, ny // 2, nz // 2)
            one_ref[part, 0:2, 0:2, a, 1:, 0:8] += add[:, :, :, 0:8]

    x2.wait_recv()
    for part in range(2):
        k2[part, 0:32] = x2_got[part * 32 : part * 32 + 32]
        for e in range(2):
            lanes = slice(e * 128, e * 128 + 128)
            k2[part, 32:40, lanes] = row_got[64 + e * 16 + part * 8 : 64 + e * 16 + part * 8 + 8]
            k2[part, 40:44, lanes] = corner_got[8 + e * 8 + part * 4 : 8 + e * 8 + part * 4 + 4]
        k2[part, 44:48] = jnp.zeros((4, nz // 2), F32)
        high, low = split(k2[part])
        grid = z_ref[3, nz : nz + 16]
        if part == 1:
            grid = jnp.zeros_like(grid)
        rest = jnp.concatenate([high, low, grid, jnp.zeros((16, nz // 2), BF16)], axis=0)
        own = t2[part] + dot(later_ref[0:144, cells:], rest)
        shape = (3, 3, nx // 4, ny // 4, nz // 4)
        two_ref[part, :, :, 1] = own[:, 0:128].reshape(shape)
        two_ref[part, :, :, 2] = own[:, 128:256].reshape(shape)
        two_ref[part, :, :, 0] = pltpu.roll(own[:, 128:256], 1, 1).reshape(shape)

    for copy in gathers:
        copy.wait_recv()
    loads[6].wait()
    shape = (3, 3, 1, sy * ny // 8, nz // 8)
    for part in range(2):
        rows = jnp.concatenate([blocks[g, part * 24 : part * 24 + 24] for g in range(sy)], axis=0)
        high, low = split(rows)
        out = dot(gather_ref[...], jnp.concatenate([high, low], axis=0))
        lane = lax.broadcasted_iota(jnp.int32, out.shape, 1)
        upper = pltpu.roll(out, 64, 1)
        lower = jnp.where(lane == 0, 0.0, pltpu.roll(out, 65, 1))
        three_ref[part, :, :, 1] = out[:, 0:64].reshape(shape)
        three_ref[part, :, :, 2] = upper[:, 0:64].reshape(shape)
        three_ref[part, :, :, 0] = lower[:, 0:64].reshape(shape)

    for copy in (plane_w, plane_a, x3, x2, row, corner, *gathers):
        copy.wait_send()


def solution(mesh):
    sx, sy = mesh.shape["gx"], mesh.shape["gy"]

    def local(wave_sq, absorb):
        nx, ny, nz = wave_sq.shape
        first, later = xy_tables(nx, ny, sx, sy)
        tables = [
            jnp.asarray(t.astype(ml_dtypes.bfloat16)) for t in (first, later, z_tables(nz), gather_table(sy, ny // 8))
        ]
        first, later, depth, gather = tables
        half = nz // 2
        return pl.pallas_call(
            functools.partial(halo_kernel, sx, sy),
            out_shape=(
                jax.ShapeDtypeStruct((2, 3, 3, 3, nx // 2, ny // 2, nz // 2), F32),
                jax.ShapeDtypeStruct((2, 3, 3, 3, nx // 4, ny // 4, nz // 4), F32),
                jax.ShapeDtypeStruct((2, 3, 3, 3, nx // 8, sy * ny // 8, nz // 8), F32),
            ),
            in_specs=[pl.BlockSpec(memory_space=pl.ANY)] * 6,
            out_specs=[pl.BlockSpec(memory_space=pltpu.VMEM)] * 3,
            scratch_shapes=[
                pltpu.VMEM((nx, ny, nz), F32),
                pltpu.VMEM((nx, ny, nz), F32),
                pltpu.VMEM(first.shape[1:], BF16),
                pltpu.VMEM(later.shape[1:], BF16),
                pltpu.VMEM(depth.shape, BF16),
                pltpu.VMEM(gather.shape, BF16),
                pltpu.VMEM((2, 2, nx * ny, nz), BF16),
                pltpu.VMEM((2, ny, nz), F32),
                pltpu.VMEM((104, 128), F32),
                pltpu.VMEM((104, 128), F32),
                pltpu.VMEM((32, 128), F32),
                pltpu.VMEM((32, 128), F32),
                pltpu.VMEM((64, half), F32),
                pltpu.VMEM((64, half), F32),
                pltpu.VMEM((32, 128), F32),
                pltpu.VMEM((32, 128), F32),
                pltpu.VMEM((sy, 48, 128), F32),
                pltpu.VMEM((2, 144, half), F32),
                pltpu.VMEM((2, 32, 128), F32),
                pltpu.VMEM((2, HALO, half), F32),
                pltpu.VMEM((2, 32, 128), F32),
                pltpu.VMEM((2, nz // 128, nx, 128), F32),
                pltpu.SemaphoreType.DMA((7,)),
                pltpu.SemaphoreType.DMA((6 + sy - 1,)),
                pltpu.SemaphoreType.DMA((6 + sy - 1,)),
            ],
            compiler_params=pltpu.CompilerParams(
                collective_id=0, has_side_effects=True, vmem_limit_bytes=32 * 1024 * 1024
            ),
        )(wave_sq, absorb, first, later, depth, gather)

    return jax.shard_map(
        local,
        mesh=mesh,
        in_specs=(P("gx", "gy", None), P("gx", "gy", None)),
        out_specs=(
            P(None, None, None, None, "gx", "gy", None),
            P(None, None, None, None, "gx", "gy", None),
            P(None, None, None, None, "gx", None, None),
        ),
        check_vma=False,
    )
```

```python
import functools

import jax
import jax.numpy as jnp
import ml_dtypes
import numpy as np
from jax import lax
from jax.experimental import pallas as pl
from jax.experimental.pallas import tpu as pltpu
from jax.sharding import PartitionSpec as P

MESH = pl.DeviceIdType.MESH
BF16 = jnp.bfloat16
F32 = jnp.float32
FIRST, MIDDLE, LAST = 0, 1, 2


def hat(distance, width):
    return np.maximum(0.0, 1.0 - np.abs(distance) / width)


def line_weights(cells, level, place):
    width = 2**level
    coarse = cells // width
    fine = np.arange(cells)[None, :]
    node = width * np.arange(coarse)[:, None]
    table = np.stack([hat(fine - node, width) * hat(fine - node - a * width, width) for a in (-1, 0, 1)])
    table /= width
    if place == LAST:
        table[2, -1] = 0.0
    return table


def tail_weights(cells, level, place):
    width = 2**level
    distance = np.arange(cells) - cells
    table = np.stack([hat(distance, width) * hat(distance + width, width), hat(distance, width) ** 2]) / width
    return table * (place != LAST)


def grid_tables(cells):
    lap = np.zeros((cells, 3))
    lap[:] = (-1.0, 2.0, -1.0)
    lap[0, 0] = lap[-1, 2] = 0.0
    one = np.zeros((cells, 3))
    one[:, 1] = 1.0

    def coarsen(band):
        coarse = band.shape[0] // 2
        out = np.zeros((coarse, 3))
        for row in range(coarse):
            for a in (-1, 0, 1):
                if not 0 <= row + a < coarse:
                    continue
                for step, weight in ((-1, 0.25), (0, 0.5), (1, 0.25)):
                    fine = 2 * row + step
                    if fine < 0:
                        continue
                    for b in (-1, 0, 1):
                        distance = abs(fine + b - 2 * (row + a))
                        spread = 1.0 if distance == 0 else 0.5 if distance == 1 else 0.0
                        out[row, a + 1] += weight * spread * band[fine, b + 1]
        return out

    tables = []
    for _ in range(3):
        lap, one = coarsen(lap), coarsen(one)
        tables.append((lap.T, one.T))
    return tables


def two_terms(table):
    high = table.astype(ml_dtypes.bfloat16).astype(np.float64)
    return high, table - high


def row_features(lap, one):
    (lh, ll), (oh, ol) = two_terms(lap), two_terms(one)
    columns = [lh, lh, ll, ll, oh, oh, ol, ol]
    return np.stack(columns + [np.zeros_like(lh)] * 8, axis=1)


def column_features(lap, one):
    (lh, ll), (oh, ol) = two_terms(lap), two_terms(one)
    rows = [oh, ol, oh, ol, lh, ll, lh, ll]
    return np.stack(rows + [np.zeros_like(lh)] * 8, axis=0)


def place_slice(table, place, cells):
    whole = table.shape[1]
    start = {FIRST: 0, MIDDLE: cells, LAST: whole - cells}[place]
    return table[:, start : start + cells]


def grid_rows(grid_x, grid_y, place_x, place_y, cells_x, cells_y):
    lap_x, one_x = (place_slice(t, place_x, cells_x)[:, None, :, None] for t in grid_x)
    lap_y, one_y = (place_slice(t, place_y, cells_y)[None, :, None, :] for t in grid_y)
    lap = (lap_x * one_y + one_x * lap_y).reshape(-1)
    one = (one_x * one_y).reshape(-1)
    return row_features(lap, one)


def padded(rows, count, width=None):
    out = np.zeros((count, rows.shape[1] if width is None else width))
    out[: rows.shape[0], : rows.shape[1]] = rows
    return out


def pair(left, right):
    both = np.einsum("aJi,bKj->abJKij", left, right)
    return both.reshape(-1, left.shape[2] * right.shape[2])


def xy_tables(nx, ny, sx, sy):
    grid_x, grid_y = grid_tables(nx * sx), grid_tables(ny * sy)
    first, later = [], []
    for px in (FIRST, MIDDLE, LAST):
        for py in (FIRST, MIDDLE, LAST):
            wx = [line_weights(nx, k, px) for k in (1, 2, 3)]
            wy = [line_weights(ny, k, py) for k in (1, 2, 3)]
            tx = [tail_weights(nx, k, px)[:, None, :] for k in (1, 2, 3)]
            ty = [tail_weights(ny, k, py)[:, None, :] for k in (1, 2, 3)]

            own = pair(wx[0], wy[0])
            head_x = np.zeros((3, nx // 2, 1))
            head_x[0:2, 0, 0] = 0.125 * (px != FIRST)
            head_y = np.zeros((3, ny // 2, 1))
            head_y[0:2, 0, 0] = 0.125 * (py != FIRST)
            halo = np.concatenate([pair(head_x, wy[0]), pair(wx[0], head_y), pair(head_x, head_y)], axis=1)
            halo = padded(halo, halo.shape[0], HALO)
            grid = grid_rows(grid_x[0], grid_y[0], px, py, nx // 2, ny // 2)
            first.append(padded(np.concatenate([own, halo, halo, grid], axis=1), own.shape[0], nx * ny + 128))

            m, n = nx // 4, ny // 4
            own = pair(wx[1], wy[1])
            send = [pair(tx[1], wy[1][1:]), pair(wx[1][1:], ty[1]), pair(tx[1], ty[1])]
            rows2 = padded(np.concatenate([own, *send]), 192)
            take = np.zeros((3, 3, m, n, HALO))
            for a in range(2):
                for j in range(n):
                    take[a, 1, 0, j, a * 2 * n + j] = 1.0
                    take[a, 2, 0, j, a * 2 * n + n + j] = 1.0
                    if j + 1 < n:
                        take[a, 0, 0, j + 1, a * 2 * n + n + j] = 1.0
                for i in range(m):
                    own_e, own_f = 4 * n + a * m + i, 4 * n + (2 + a) * m + i
                    take[1, a, i, 0, own_e] = 1.0
                    take[2, a, i, 0, own_f] = 1.0
                    if i + 1 < m:
                        take[0, a, i + 1, 0, own_f] = 1.0
                for b in range(2):
                    take[a, b, 0, 0, 4 * n + 4 * m + 2 * a + b] = 1.0
            take = take.reshape(-1, HALO)
            grid = grid_rows(grid_x[1], grid_y[1], px, py, m, n)
            take2 = np.concatenate([take, take, grid], axis=1)

            n = ny // 8
            own = padded(pair(wx[2], wy[2][1:]), 32)
            send = [pair(tx[2], wy[2][1:]), pair(wx[2][1:], ty[2]), pair(tx[2], ty[2])]
            rows3 = padded(np.concatenate([own, *send]), 64)
            take = np.zeros((3, 2, n, 32))
            for a in range(2):
                for e in range(2):
                    for j in range(n):
                        take[a, e, j, (a * 2 + e) * n + j] = 1.0
                take[1 + a, 0, 0, 4 * n + 2 * a + 1] = 1.0
                take[a, 0, 0, 4 * n + 4 + 2 * a + 1] = 1.0
            take = take.reshape(-1, 32)
            grid = grid_rows(grid_x[2], grid_y[2], px, py, 1, n).reshape(3, 3, n, 16)[:, 1:].reshape(-1, 16)
            take3 = np.concatenate([take, take, grid], axis=1)

            table = np.zeros((320, nx * ny + 128))
            high, low = two_terms(rows3)
            table[:, : nx * ny] = np.concatenate([rows2, high, low])
            table[: take2.shape[0], nx * ny : nx * ny + take2.shape[1]] = take2
            table[192 : 192 + take3.shape[0], nx * ny : nx * ny + take3.shape[1]] = take3
            later.append(table)
    return np.stack(first), np.stack(later)


def z_tables(nz):
    grid = grid_tables(nz)
    half = nz // 2
    blocks = []
    one = line_weights(nz, 1, LAST)
    one[0, 0] = 0.0
    for a in range(3):
        blocks.append(np.concatenate([one[a].T, column_features(grid[0][0][a], grid[0][1][a])]))
    for k in (2, 3):
        table = line_weights(nz, k, LAST)
        columns = [
            np.concatenate([table[a].T, column_features(grid[k - 1][0][a], grid[k - 1][1][a])]) for a in (1, 2)
        ]
        block = np.concatenate(columns, axis=1)
        blocks.append(padded(block, nz + 16, half))
    return np.stack(blocks)


def gather_table(parts, n):
    table = np.zeros((3, 3, parts * n, parts, 3, 2, n))
    for a in range(3):
        for g in range(parts):
            for j in range(n):
                row = g * n + j
                table[a, 1, row, g, a, 0, j] = 1.0
                table[a, 2, row, g, a, 1, j] = 1.0
                if row + 1 < parts * n:
                    table[a, 0, row + 1, g, a, 1, j] = 1.0
    table = table.reshape(9 * parts * n, -1)
    return np.concatenate([table, table], axis=1)


HALO = 48


def split(value):
    high = value.astype(BF16)
    return high, (value - high.astype(F32)).astype(BF16)


def dot(left, right):
    return jnp.dot(left, right, preferred_element_type=F32)


def exact_dot(left, value):
    high, low = split(value)
    return dot(left, high) + dot(left, low)


def halo_kernel(
    sx, sy,
    w_hbm, a_hbm, first_hbm, later_hbm, z_hbm, gather_hbm,
    one_ref, t2_ref, x2_ref, three_ref,
    w_ref, a_ref, first_ref, later_ref, z_ref, gather_ref,
    mass, plane, row_send, row_got, corner_send, corner_got,
    x2_send, x2_got, x3_send, x3_got, blocks, t2, t3, k2, k3, raw,
    load_sem, send_sem, got_sem,
):
    ix, iy = lax.axis_index("gx"), lax.axis_index("gy")
    nx, ny, nz = w_hbm.shape
    cells = nx * ny
    next_x, last_x = lax.rem(ix + 1, sx), lax.rem(ix + sx - 1, sx)
    next_y, last_y = lax.rem(iy + 1, sy), lax.rem(iy + sy - 1, sy)
    from_x, to_x, from_y, to_y = ix > 0, ix < sx - 1, iy > 0, iy < sy - 1
    from_xy, to_xy = from_x & from_y, to_x & to_y
    peers = [lax.rem(iy + step, sy) for step in range(1, sy)]

    place_x = jnp.where(ix == 0, FIRST, jnp.where(ix == sx - 1, LAST, MIDDLE))
    place_y = jnp.where(iy == 0, FIRST, jnp.where(iy == sy - 1, LAST, MIDDLE))
    place = place_x * 3 + place_y
    loads = [
        pltpu.make_async_copy(src, dst, load_sem.at[i])
        for i, (src, dst) in enumerate(
            (
                (w_hbm, w_ref),
                (a_hbm, a_ref),
                (later_hbm.at[place], later_ref),
                (z_hbm.at[pl.ds(3, 2)], z_ref.at[pl.ds(3, 2)]),
                (z_hbm.at[pl.ds(0, 3)], z_ref.at[pl.ds(0, 3)]),
                (first_hbm.at[place], first_ref),
                (gather_hbm, gather_ref),
            )
        )
    ]
    for load in loads:
        load.start()

    @pl.when(jnp.logical_not(from_x))
    def _():
        plane[...] = jnp.zeros_like(plane)
        x2_got[...] = jnp.zeros_like(x2_got)
        x3_got[...] = jnp.zeros_like(x3_got)

    @pl.when(jnp.logical_not(from_y))
    def _():
        row_got[...] = jnp.zeros_like(row_got)

    @pl.when(jnp.logical_not(from_xy))
    def _():
        corner_got[...] = jnp.zeros_like(corner_got)

    def signal(*device):
        pl.semaphore_signal(barrier, inc=1, device_id=device, device_id_type=MESH)

    barrier = pltpu.get_barrier_semaphore()
    for p in peers:
        signal(ix, p)
    pl.when(from_x)(lambda: signal(last_x, iy))
    pl.when(from_xy)(lambda: signal(last_x, last_y))
    pl.semaphore_wait(barrier, sy - 1 + to_x.astype(jnp.int32) + to_xy.astype(jnp.int32))

    def remote(slot, src, dst, device):
        return pltpu.make_async_remote_copy(
            src_ref=src, dst_ref=dst, send_sem=send_sem.at[slot], recv_sem=got_sem.at[slot],
            device_id=device, device_id_type=MESH,
        )

    plane_w = remote(0, w_hbm.at[nx - 1], plane.at[0], (next_x, iy))
    plane_a = remote(1, a_hbm.at[nx - 1], plane.at[1], (next_x, iy))
    x3 = remote(2, x3_send, x3_got, (next_x, iy))
    x2 = remote(3, x2_send, x2_got, (next_x, iy))
    row = remote(4, row_send, row_got, (ix, next_y))
    corner = remote(5, corner_send, corner_got, (next_x, next_y))
    gathers = [remote(6 + i, blocks.at[iy], blocks.at[iy], (ix, p)) for i, p in enumerate(peers)]

    @pl.when(to_x)
    def _():
        plane_w.start()
        plane_a.start()

    loads[0].wait()
    loads[1].wait()
    for x in range(nx):
        w, a = w_ref[x], a_ref[x]
        for part, value in enumerate((-(w + 0.5 * a), 0.5 * w - a)):
            high, low = split(value)
            mass[part, 0, x * ny : (x + 1) * ny] = high
            mass[part, 1, x * ny : (x + 1) * ny] = low
            for c in range(nz // 128):
                raw[part, c, x : x + 1] = value[ny - 1 : ny, c * 128 : (c + 1) * 128]
    loads[2].wait()
    loads[3].wait()

    for part in range(2):
        table = later_ref[:, 0:cells]
        rows = dot(table, mass[part, 0]) + dot(table, mass[part, 1])
        high, low = split(rows[0:192])
        two = dot(high, z_ref[3, 0:nz]) + dot(low, z_ref[3, 0:nz])
        high, low = split(rows[192:256] + rows[256:320])
        three = dot(high, z_ref[4, 0:nz, 0:128]) + dot(low, z_ref[4, 0:nz, 0:128])
        t2[part] = two[0:144]
        t3[part] = three[0:32]
        x3_send[part * 16 : part * 16 + 16] = three[32:48]
        x2_send[part * 32 : part * 32 + 32] = two[144:176]
        for e in range(2):
            row_send[64 + e * 16 + part * 8 : 64 + e * 16 + part * 8 + 8] = two[176:184, e * 128 : e * 128 + 128]
            corner_send[8 + e * 8 + part * 4 : 8 + e * 8 + part * 4 + 4] = two[184:188, e * 128 : e * 128 + 128]
        row_send[96 + part * 4 : 96 + part * 4 + 4] = three[48:52]
        corner_send[24 + part * 4 : 24 + part * 4 + 4] = three[52:56]
        for c in range(nz // 128):
            row_send[part * 32 + c * 8 : part * 32 + c * 8 + 8] = raw[part, c]
            corner_send[part * 4 + c : part * 4 + c + 1] = raw[part, c, nx - 1 : nx]

    @pl.when(to_x)
    def _():
        x3.start()
        x2.start()

    pl.when(to_y)(row.start)
    pl.when(to_xy)(corner.start)

    loads[4].wait()
    loads[5].wait()

    def own_level_one(i, carry):
        part, a = i // 3, lax.rem(i, 3)
        table = z_ref[a]
        z = dot(mass[part, 0], table[0:nz]) + dot(mass[part, 1], table[0:nz])
        high, low = split(z)
        grid = jnp.where(part == 0, table[nz : nz + 16], jnp.zeros((16, nz // 2), BF16))
        rest = jnp.concatenate([jnp.zeros((2 * HALO, nz // 2), BF16), grid, jnp.zeros((16, nz // 2), BF16)], axis=0)
        for ax in range(3):
            rows = first_ref[ax * 192 : ax * 192 + 192]
            out = dot(rows[:, 0:cells], high) + dot(rows[:, 0:cells], low) + dot(rows[:, cells:], rest)
            one_ref[part, ax, :, a] = out.reshape(3, nx // 2, ny // 2, nz // 2)
        return carry

    lax.fori_loop(0, 6, own_level_one, 0)

    pl.when(from_y)(row.wait_recv)
    pl.when(from_xy)(corner.wait_recv)
    pl.when(from_x)(x3.wait_recv)
    for part in range(2):
        k3[part, 0:16] = x3_got[part * 16 : part * 16 + 16]
        k3[part, 16:20] = row_got[96 + part * 4 : 96 + part * 4 + 4]
        k3[part, 20:24] = corner_got[24 + part * 4 : 24 + part * 4 + 4]
        k3[part, 24:32] = jnp.zeros((8, 128), F32)
        high, low = split(k3[part])
        grid = z_ref[4, nz : nz + 16, 0:128]
        if part == 1:
            grid = jnp.zeros_like(grid)
        rest = jnp.concatenate([high, low, grid, jnp.zeros((48, 128), BF16)], axis=0)
        own = t3[part] + dot(later_ref[192:224, cells:], rest)
        blocks[iy, part * 24 : part * 24 + 24] = own[0:24]
    for copy in gathers:
        copy.start()

    for part in range(2):
        k2[part, 0:32] = jnp.zeros((32, nz // 2), F32)
        for e in range(2):
            lanes = slice(e * 128, e * 128 + 128)
            k2[part, 32:40, lanes] = row_got[64 + e * 16 + part * 8 : 64 + e * 16 + part * 8 + 8]
            k2[part, 40:44, lanes] = corner_got[8 + e * 8 + part * 4 : 8 + e * 8 + part * 4 + 4]
        k2[part, 44:48] = jnp.zeros((4, nz // 2), F32)
        high, low = split(k2[part])
        grid = z_ref[3, nz : nz + 16]
        if part == 1:
            grid = jnp.zeros_like(grid)
        rest = jnp.concatenate([high, low, grid, jnp.zeros((16, nz // 2), BF16)], axis=0)
        t2_ref[part] = t2[part] + dot(later_ref[0:144, cells:], rest)


    @pl.when(from_x)
    def _():
        plane_w.wait_recv()
        plane_a.wait_recv()

    for part in range(2):
        w, a = plane[0], plane[1]
        value = -(w + 0.5 * a) if part == 0 else 0.5 * w - a
        rows = jnp.concatenate([row_got[part * 32 + c * 8 : part * 32 + c * 8 + 8] for c in range(nz // 128)], axis=1)
        edge = jnp.concatenate([corner_got[part * 4 + c : part * 4 + c + 1] for c in range(nz // 128)], axis=1)
        high, low = split(jnp.concatenate([value, rows, edge, jnp.zeros((7, nz), F32)], axis=0))
        for a in range(3):
            z = dot(high, z_ref[a, 0:nz]) + dot(low, z_ref[a, 0:nz])
            zh, zl = split(z)
            rest = jnp.concatenate([zh, zl, jnp.zeros((32, nz // 2), BF16)], axis=0)
            table = first_ref[:, cells:].reshape(3, 3, nx // 2, ny // 2, 128)
            add = dot(table[0:2, :, 0].reshape(-1, 128), rest)
            one_ref[part, 0:2, :, a, 0] += add.reshape(2, 3, ny // 2, nz // 2)
            add = dot(table[2, 0:2].reshape(-1, 128), rest).reshape(2, nx // 2, ny // 2, nz // 2)
            one_ref[part, 2, 0:2, a, :, 0:8] += add[:, :, 0:8]
            add = dot(table[0:2, 0:2, 1:].reshape(-1, 128), rest).reshape(2, 2, nx // 2 - 1, ny // 2, nz // 2)
            one_ref[part, 0:2, 0:2, a, 1:, 0:8] += add[:, :, :, 0:8]

    for copy in gathers:
        copy.wait_recv()
    loads[6].wait()
    shape = (3, 3, 1, sy * ny // 8, nz // 8)
    for part in range(2):
        rows = jnp.concatenate([blocks[g, part * 24 : part * 24 + 24] for g in range(sy)], axis=0)
        high, low = split(rows)
        out = dot(gather_ref[...], jnp.concatenate([high, low], axis=0))
        lane = lax.broadcasted_iota(jnp.int32, out.shape, 1)
        upper = pltpu.roll(out, 64, 1)
        lower = jnp.where(lane == 0, 0.0, pltpu.roll(out, 65, 1))
        three_ref[part, :, :, 1] = out[:, 0:64].reshape(shape)
        three_ref[part, :, :, 2] = upper[:, 0:64].reshape(shape)
        three_ref[part, :, :, 0] = lower[:, 0:64].reshape(shape)

    pl.when(from_x)(x2.wait_recv)
    x2_ref[...] = x2_got[...]

    for copy in gathers:
        copy.wait_send()
    pl.when(to_y)(row.wait_send)
    pl.when(to_xy)(corner.wait_send)

    @pl.when(to_x)
    def _():
        for copy in (plane_w, plane_a, x3, x2):
            copy.wait_send()


def result_kernel(one_ref, t2_ref, x2_ref, three_ref, one_hbm, two_hbm, three_hbm, two, sem):
    ones = [
        pltpu.make_async_copy(one_ref.at[part, a], one_hbm.at[part, a], sem.at[3 * part + a])
        for part in range(2)
        for a in range(3)
    ]
    three = pltpu.make_async_copy(three_ref, three_hbm, sem.at[6])
    three.start()
    for copy in ones:
        copy.start()
    _, _, _, _, m, n, depth = two.shape
    for part in range(2):
        whole = t2_ref[part].reshape(3, 3, m, n, 2 * depth)
        for a in range(3):
            for b in range(3):
                for x in range(m):
                    value = whole[a, b, x]
                    if x == 0 and a < 2:
                        base = part * 32 + a * 2 * n
                        if b > 0:
                            value = value + x2_ref[base + (b - 1) * n : base + b * n]
                        else:
                            above = pltpu.roll(x2_ref[base + n : base + 2 * n], 1, 0)
                            line = lax.broadcasted_iota(jnp.int32, above.shape, 0)
                            value = value + jnp.where(line == 0, 0.0, above)
                    two[part, a, b, 1, x] = value[:, 0:depth]
                    two[part, a, b, 2, x] = value[:, depth:]
                    two[part, a, b, 0, x] = pltpu.roll(value[:, depth:], 1, 1)
    copy = pltpu.make_async_copy(two, two_hbm, sem.at[7])
    copy.start()
    for done in (three, *ones, copy):
        done.wait()


def solution(mesh):
    sx, sy = mesh.shape["gx"], mesh.shape["gy"]

    def local(wave_sq, absorb):
        nx, ny, nz = wave_sq.shape
        first, later = xy_tables(nx, ny, sx, sy)
        tables = [
            jnp.asarray(t.astype(ml_dtypes.bfloat16)) for t in (first, later, z_tables(nz), gather_table(sy, ny // 8))
        ]
        first, later, depth, gather = tables
        half = nz // 2
        level_one = jax.ShapeDtypeStruct((2, 3, 3, 3, nx // 2, ny // 2, nz // 2), F32)
        level_two = jax.ShapeDtypeStruct((2, 3, 3, 3, nx // 4, ny // 4, nz // 4), F32)
        level_three = jax.ShapeDtypeStruct((2, 3, 3, 3, nx // 8, sy * ny // 8, nz // 8), F32)
        parts = pl.pallas_call(
            functools.partial(halo_kernel, sx, sy),
            out_shape=(
                level_one,
                jax.ShapeDtypeStruct((2, 144, half), F32),
                jax.ShapeDtypeStruct((64, half), F32),
                level_three,
            ),
            in_specs=[pl.BlockSpec(memory_space=pltpu.HBM)] * 6,
            out_specs=[pl.BlockSpec(memory_space=pltpu.VMEM)] * 4,
            scratch_shapes=[
                pltpu.VMEM((nx, ny, nz), F32),
                pltpu.VMEM((nx, ny, nz), F32),
                pltpu.VMEM(first.shape[1:], BF16),
                pltpu.VMEM(later.shape[1:], BF16),
                pltpu.VMEM(depth.shape, BF16),
                pltpu.VMEM(gather.shape, BF16),
                pltpu.VMEM((2, 2, nx * ny, nz), BF16),
                pltpu.VMEM((2, ny, nz), F32),
                pltpu.VMEM((104, 128), F32),
                pltpu.VMEM((104, 128), F32),
                pltpu.VMEM((32, 128), F32),
                pltpu.VMEM((32, 128), F32),
                pltpu.VMEM((64, half), F32),
                pltpu.VMEM((64, half), F32),
                pltpu.VMEM((32, 128), F32),
                pltpu.VMEM((32, 128), F32),
                pltpu.VMEM((sy, 48, 128), F32),
                pltpu.VMEM((2, 144, half), F32),
                pltpu.VMEM((2, 32, 128), F32),
                pltpu.VMEM((2, HALO, half), F32),
                pltpu.VMEM((2, 32, 128), F32),
                pltpu.VMEM((2, nz // 128, nx, 128), F32),
                pltpu.SemaphoreType.DMA((7,)),
                pltpu.SemaphoreType.DMA((6 + sy - 1,)),
                pltpu.SemaphoreType.DMA((6 + sy - 1,)),
            ],
            compiler_params=pltpu.CompilerParams(
                collective_id=0, has_side_effects=True, vmem_limit_bytes=32 * 1024 * 1024
            ),
        )(*[pltpu.with_memory_space_constraint(v, pltpu.HBM) for v in (wave_sq, absorb, first, later, depth, gather)])
        return pl.pallas_call(
            result_kernel,
            out_shape=(level_one, level_two, level_three),
            in_specs=[pl.BlockSpec(memory_space=pltpu.VMEM)] * 4,
            out_specs=[pl.BlockSpec(memory_space=pltpu.HBM)] * 3,
            scratch_shapes=[pltpu.VMEM(level_two.shape, F32), pltpu.SemaphoreType.DMA((8,))],
            compiler_params=pltpu.CompilerParams(vmem_limit_bytes=16 * 1024 * 1024),
        )(*parts)

    return jax.shard_map(
        local,
        mesh=mesh,
        in_specs=(P("gx", "gy", None), P("gx", "gy", None)),
        out_specs=(
            P(None, None, None, None, "gx", "gy", None),
            P(None, None, None, None, "gx", "gy", None),
            P(None, None, None, None, "gx", None, None),
        ),
        check_vma=False,
    )
```

```python
import functools

import jax
import jax.numpy as jnp
import ml_dtypes
import numpy as np
from jax import lax
from jax.experimental import pallas as pl
from jax.experimental.pallas import tpu as pltpu
from jax.sharding import PartitionSpec as P

MESH = pl.DeviceIdType.MESH
BF16 = jnp.bfloat16
F32 = jnp.float32
FIRST, MIDDLE, LAST = 0, 1, 2


def hat(distance, width):
    return np.maximum(0.0, 1.0 - np.abs(distance) / width)


def line_weights(cells, level, place):
    width = 2**level
    coarse = cells // width
    fine = np.arange(cells)[None, :]
    node = width * np.arange(coarse)[:, None]
    table = np.stack([hat(fine - node, width) * hat(fine - node - a * width, width) for a in (-1, 0, 1)])
    table /= width
    if place == LAST:
        table[2, -1] = 0.0
    return table


def tail_weights(cells, level, place):
    width = 2**level
    distance = np.arange(cells) - cells
    table = np.stack([hat(distance, width) * hat(distance + width, width), hat(distance, width) ** 2]) / width
    return table * (place != LAST)


def grid_tables(cells):
    lap = np.zeros((cells, 3))
    lap[:] = (-1.0, 2.0, -1.0)
    lap[0, 0] = lap[-1, 2] = 0.0
    one = np.zeros((cells, 3))
    one[:, 1] = 1.0

    def coarsen(band):
        coarse = band.shape[0] // 2
        out = np.zeros((coarse, 3))
        for row in range(coarse):
            for a in (-1, 0, 1):
                if not 0 <= row + a < coarse:
                    continue
                for step, weight in ((-1, 0.25), (0, 0.5), (1, 0.25)):
                    fine = 2 * row + step
                    if fine < 0:
                        continue
                    for b in (-1, 0, 1):
                        distance = abs(fine + b - 2 * (row + a))
                        spread = 1.0 if distance == 0 else 0.5 if distance == 1 else 0.0
                        out[row, a + 1] += weight * spread * band[fine, b + 1]
        return out

    tables = []
    for _ in range(3):
        lap, one = coarsen(lap), coarsen(one)
        tables.append((lap.T, one.T))
    return tables


def two_terms(table):
    high = table.astype(ml_dtypes.bfloat16).astype(np.float64)
    return high, table - high


def row_features(lap, one):
    (lh, ll), (oh, ol) = two_terms(lap), two_terms(one)
    columns = [lh, lh, ll, ll, oh, oh, ol, ol]
    return np.stack(columns + [np.zeros_like(lh)] * 8, axis=1)


def column_features(lap, one):
    (lh, ll), (oh, ol) = two_terms(lap), two_terms(one)
    rows = [oh, ol, oh, ol, lh, ll, lh, ll]
    return np.stack(rows + [np.zeros_like(lh)] * 8, axis=0)


def place_slice(table, place, cells):
    whole = table.shape[1]
    start = {FIRST: 0, MIDDLE: cells, LAST: whole - cells}[place]
    return table[:, start : start + cells]


def grid_rows(grid_x, grid_y, place_x, place_y, cells_x, cells_y):
    lap_x, one_x = (place_slice(t, place_x, cells_x)[:, None, :, None] for t in grid_x)
    lap_y, one_y = (place_slice(t, place_y, cells_y)[None, :, None, :] for t in grid_y)
    lap = (lap_x * one_y + one_x * lap_y).reshape(-1)
    one = (one_x * one_y).reshape(-1)
    return row_features(lap, one)


def padded(rows, count, width=None):
    out = np.zeros((count, rows.shape[1] if width is None else width))
    out[: rows.shape[0], : rows.shape[1]] = rows
    return out


def pair(left, right):
    both = np.einsum("aJi,bKj->abJKij", left, right)
    return both.reshape(-1, left.shape[2] * right.shape[2])


def xy_tables(nx, ny, sx, sy):
    grid_x, grid_y = grid_tables(nx * sx), grid_tables(ny * sy)
    first, later = [], []
    for px in (FIRST, MIDDLE, LAST):
        for py in (FIRST, MIDDLE, LAST):
            wx = [line_weights(nx, k, px) for k in (1, 2, 3)]
            wy = [line_weights(ny, k, py) for k in (1, 2, 3)]
            tx = [tail_weights(nx, k, px)[:, None, :] for k in (1, 2, 3)]
            ty = [tail_weights(ny, k, py)[:, None, :] for k in (1, 2, 3)]

            own = pair(wx[0], wy[0])
            head_x = np.zeros((3, nx // 2, 1))
            head_x[0:2, 0, 0] = 0.125 * (px != FIRST)
            head_y = np.zeros((3, ny // 2, 1))
            head_y[0:2, 0, 0] = 0.125 * (py != FIRST)
            halo = np.concatenate([pair(head_x, wy[0]), pair(wx[0], head_y), pair(head_x, head_y)], axis=1)
            halo = padded(halo, halo.shape[0], HALO)
            grid = grid_rows(grid_x[0], grid_y[0], px, py, nx // 2, ny // 2)
            first.append(padded(np.concatenate([own, halo, halo, grid], axis=1), own.shape[0], nx * ny + 128))

            m, n = nx // 4, ny // 4
            own = pair(wx[1], wy[1])
            send = [pair(tx[1], wy[1][1:]), pair(wx[1][1:], ty[1]), pair(tx[1], ty[1])]
            rows2 = padded(np.concatenate([own, *send]), 192)
            take = np.zeros((3, 3, m, n, HALO))
            for a in range(2):
                for j in range(n):
                    take[a, 1, 0, j, a * 2 * n + j] = 1.0
                    take[a, 2, 0, j, a * 2 * n + n + j] = 1.0
                    if j + 1 < n:
                        take[a, 0, 0, j + 1, a * 2 * n + n + j] = 1.0
                for i in range(m):
                    own_e, own_f = 4 * n + a * m + i, 4 * n + (2 + a) * m + i
                    take[1, a, i, 0, own_e] = 1.0
                    take[2, a, i, 0, own_f] = 1.0
                    if i + 1 < m:
                        take[0, a, i + 1, 0, own_f] = 1.0
                for b in range(2):
                    take[a, b, 0, 0, 4 * n + 4 * m + 2 * a + b] = 1.0
            take = take.reshape(-1, HALO)
            grid = grid_rows(grid_x[1], grid_y[1], px, py, m, n)
            take2 = np.concatenate([take, take, grid], axis=1)

            n = ny // 8
            own = padded(pair(wx[2], wy[2][1:]), 32)
            send = [pair(tx[2], wy[2][1:]), pair(wx[2][1:], ty[2]), pair(tx[2], ty[2])]
            rows3 = padded(np.concatenate([own, *send]), 64)
            take = np.zeros((3, 2, n, 32))
            for a in range(2):
                for e in range(2):
                    for j in range(n):
                        take[a, e, j, (a * 2 + e) * n + j] = 1.0
                take[1 + a, 0, 0, 4 * n + 2 * a + 1] = 1.0
                take[a, 0, 0, 4 * n + 4 + 2 * a + 1] = 1.0
            take = take.reshape(-1, 32)
            grid = grid_rows(grid_x[2], grid_y[2], px, py, 1, n).reshape(3, 3, n, 16)[:, 1:].reshape(-1, 16)
            take3 = np.concatenate([take, take, grid], axis=1)

            table = np.zeros((320, nx * ny + 128))
            high, low = two_terms(rows3)
            table[:, : nx * ny] = np.concatenate([rows2, high, low])
            table[: take2.shape[0], nx * ny : nx * ny + take2.shape[1]] = take2
            table[192 : 192 + take3.shape[0], nx * ny : nx * ny + take3.shape[1]] = take3
            later.append(table)
    return np.stack(first), np.stack(later)


def z_tables(nz):
    grid = grid_tables(nz)
    half = nz // 2
    blocks = []
    one = line_weights(nz, 1, LAST)
    one[0, 0] = 0.0
    for a in range(3):
        blocks.append(np.concatenate([one[a].T, column_features(grid[0][0][a], grid[0][1][a])]))
    for k in (2, 3):
        table = line_weights(nz, k, LAST)
        columns = [
            np.concatenate([table[a].T, column_features(grid[k - 1][0][a], grid[k - 1][1][a])]) for a in (1, 2)
        ]
        block = np.concatenate(columns, axis=1)
        blocks.append(padded(block, nz + 16, half))
    return np.stack(blocks)


def gather_table(parts, n):
    table = np.zeros((3, 3, parts * n, parts, 3, 2, n))
    for a in range(3):
        for g in range(parts):
            for j in range(n):
                row = g * n + j
                table[a, 1, row, g, a, 0, j] = 1.0
                table[a, 2, row, g, a, 1, j] = 1.0
                if row + 1 < parts * n:
                    table[a, 0, row + 1, g, a, 1, j] = 1.0
    table = table.reshape(9 * parts * n, -1)
    return np.concatenate([table, table], axis=1)


HALO = 48
TURNS = 4


def split(value):
    high = value.astype(BF16)
    return high, (value - high.astype(F32)).astype(BF16)


def dot(left, right):
    return jnp.dot(left, right, preferred_element_type=F32)


def exact_dot(left, value):
    high, low = split(value)
    return dot(left, high) + dot(left, low)


def halo_kernel(
    sx, sy,
    w_hbm, a_hbm, first_hbm, later_hbm, z_hbm, gather_hbm,
    one_ref, t2_ref, x2_got, blocks, plane, edge, z_ref, head_ref, gather_ref,
    w_ref, a_ref, first_ref, later_ref, later_z_ref,
    mass, row_send, row_got, corner_send, corner_got,
    x2_send, x3_send, x3_got, t2, t3, k2, k3, raw, through,
    load_sem, send_sem, got_sem,
):
    ix, iy = lax.axis_index("gx"), lax.axis_index("gy")
    nx, ny, nz = w_hbm.shape
    cells = nx * ny
    next_x, last_x = lax.rem(ix + 1, sx), lax.rem(ix + sx - 1, sx)
    next_y, last_y = lax.rem(iy + 1, sy), lax.rem(iy + sy - 1, sy)
    from_x, to_x, from_y, to_y = ix > 0, ix < sx - 1, iy > 0, iy < sy - 1
    from_xy, to_xy = from_x & from_y, to_x & to_y
    turn = sx // TURNS
    turning = sx == TURNS * 32
    at = lax.rem(ix, turn)
    leads = to_x & (at == turn - 1) & turning
    helps = (ix < sx - turn) & (at == 3) & turning
    waits = from_x & (at == 0) & turning
    peers = [lax.rem(iy + step, sy) for step in range(1, sy)]

    place_x = jnp.where(ix == 0, FIRST, jnp.where(ix == sx - 1, LAST, MIDDLE))
    place_y = jnp.where(iy == 0, FIRST, jnp.where(iy == sy - 1, LAST, MIDDLE))
    place = place_x * 3 + place_y
    loads = [
        pltpu.make_async_copy(src, dst, load_sem.at[i])
        for i, (src, dst) in enumerate(
            (
                (w_hbm, w_ref),
                (a_hbm, a_ref),
                (later_hbm.at[place], later_ref),
                (z_hbm.at[pl.ds(3, 2)], later_z_ref),
                (z_hbm.at[pl.ds(0, 3)], z_ref),
                (first_hbm.at[place], first_ref),
                (gather_hbm, gather_ref),
            )
        )
    ]
    for load in loads[:4]:
        load.start()

    @pl.when(jnp.logical_not(from_x))
    def _():
        plane[...] = jnp.zeros_like(plane)
        x2_got[...] = jnp.zeros_like(x2_got)
        x3_got[...] = jnp.zeros_like(x3_got)

    @pl.when(jnp.logical_not(from_y))
    def _():
        row_got[...] = jnp.zeros_like(row_got)

    @pl.when(jnp.logical_not(from_xy))
    def _():
        corner_got[...] = jnp.zeros_like(corner_got)

    def signal(*device):
        pl.semaphore_signal(barrier, inc=1, device_id=device, device_id_type=MESH)

    barrier = pltpu.get_barrier_semaphore()
    for p in peers:
        signal(ix, p)
    pl.when(from_x)(lambda: signal(last_x, iy))
    pl.when(from_xy)(lambda: signal(last_x, last_y))
    pl.when(waits)(lambda: signal(ix - turn + 3, iy))
    pl.when(helps)(lambda: signal(ix + turn - 4, iy))
    sends_to = [flag.astype(jnp.int32) for flag in (to_x, to_xy, leads, helps)]
    pl.semaphore_wait(barrier, sy - 1 + sum(sends_to))

    def remote(slot, src, dst, device, got=None):
        got = slot if got is None else got
        return pltpu.make_async_remote_copy(
            src_ref=src, dst_ref=dst, send_sem=send_sem.at[slot], recv_sem=got_sem.at[got],
            device_id=device, device_id_type=MESH,
        )

    plane_w = remote(0, w_hbm.at[nx - 1], plane.at[0], (next_x, iy))
    plane_a = remote(1, a_hbm.at[nx - 1], plane.at[1], (next_x, iy))
    x3 = remote(2, x3_send, x3_got, (next_x, iy))
    x2 = remote(3, x2_send, x2_got, (next_x, iy))
    row = remote(4, row_send, row_got, (ix, next_y))
    corner = remote(5, corner_send, corner_got, (next_x, next_y))
    gathers = [remote(6 + i, blocks.at[iy], blocks.at[iy], (ix, p)) for i, p in enumerate(peers)]

    lead = remote(5 + sy, a_hbm.at[nx - 1], through, (jnp.maximum(ix - turn + 4, 0), iy))
    follow = remote(6 + sy, through, plane.at[1], (jnp.minimum(ix + turn - 3, sx - 1), iy), got=1)

    pl.when(to_x)(plane_w.start)
    pl.when(leads)(lead.start)
    for load in loads[4:]:
        load.start()

    loads[0].wait()
    loads[1].wait()
    for x in range(nx):
        w, a = w_ref[x], a_ref[x]
        for part, value in enumerate((-(w + 0.5 * a), 0.5 * w - a)):
            high, low = split(value)
            mass[part, 0, x * ny : (x + 1) * ny] = high
            mass[part, 1, x * ny : (x + 1) * ny] = low
            for c in range(nz // 128):
                raw[part, c, x : x + 1] = value[ny - 1 : ny, c * 128 : (c + 1) * 128]
    loads[2].wait()
    loads[3].wait()

    for part in range(2):
        table = later_ref[:, 0:cells]
        rows = dot(table, mass[part, 0]) + dot(table, mass[part, 1])
        high, low = split(rows[0:192])
        two = dot(high, later_z_ref[0, 0:nz]) + dot(low, later_z_ref[0, 0:nz])
        high, low = split(rows[192:256] + rows[256:320])
        three = dot(high, later_z_ref[1, 0:nz, 0:128]) + dot(low, later_z_ref[1, 0:nz, 0:128])
        t2[part] = two[0:144]
        t3[part] = three[0:32]
        x3_send[part * 16 : part * 16 + 16] = three[32:48]
        x2_send[part * 32 : part * 32 + 32] = two[144:176]
        for e in range(2):
            row_send[64 + e * 16 + part * 8 : 64 + e * 16 + part * 8 + 8] = two[176:184, e * 128 : e * 128 + 128]
            corner_send[8 + e * 8 + part * 4 : 8 + e * 8 + part * 4 + 4] = two[184:188, e * 128 : e * 128 + 128]
        row_send[96 + part * 4 : 96 + part * 4 + 4] = three[48:52]
        corner_send[24 + part * 4 : 24 + part * 4 + 4] = three[52:56]
        for c in range(nz // 128):
            row_send[part * 32 + c * 8 : part * 32 + c * 8 + 8] = raw[part, c]
            corner_send[part * 4 + c : part * 4 + c + 1] = raw[part, c, nx - 1 : nx]

    pl.when(to_x)(x3.start)
    pl.when(to_xy)(corner.start)
    pl.when(to_y)(row.start)

    pl.when(to_x & jnp.logical_not(leads))(plane_a.start)
    pl.when(to_x)(x2.start)

    loads[4].wait()
    loads[5].wait()

    def own_level_one(i, carry):
        part, a = i // 3, lax.rem(i, 3)
        table = z_ref[a]
        z = dot(mass[part, 0], table[0:nz]) + dot(mass[part, 1], table[0:nz])
        high, low = split(z)
        grid = jnp.where(part == 0, table[nz : nz + 16], jnp.zeros((16, nz // 2), BF16))
        rest = jnp.concatenate([jnp.zeros((2 * HALO, nz // 2), BF16), grid, jnp.zeros((16, nz // 2), BF16)], axis=0)
        for ax in range(3):
            rows = first_ref[ax * 192 : ax * 192 + 192]
            out = dot(rows[:, 0:cells], high) + dot(rows[:, 0:cells], low) + dot(rows[:, cells:], rest)
            one_ref[part, ax, :, a] = out.reshape(3, nx // 2, ny // 2, nz // 2)
        return carry

    lax.fori_loop(0, 6, own_level_one, 0)

    pl.when(from_y)(row.wait_recv)
    pl.when(from_xy)(corner.wait_recv)
    pl.when(from_x)(x3.wait_recv)
    for part in range(2):
        k3[part, 0:16] = x3_got[part * 16 : part * 16 + 16]
        k3[part, 16:20] = row_got[96 + part * 4 : 96 + part * 4 + 4]
        k3[part, 20:24] = corner_got[24 + part * 4 : 24 + part * 4 + 4]
        k3[part, 24:32] = jnp.zeros((8, 128), F32)
        high, low = split(k3[part])
        grid = later_z_ref[1, nz : nz + 16, 0:128]
        if part == 1:
            grid = jnp.zeros_like(grid)
        rest = jnp.concatenate([high, low, grid, jnp.zeros((48, 128), BF16)], axis=0)
        own = t3[part] + dot(later_ref[192:224, cells:], rest)
        blocks[iy, part * 24 : part * 24 + 24] = own[0:24]
    for copy in gathers:
        copy.start()

    for part in range(2):
        k2[part, 0:32] = jnp.zeros((32, nz // 2), F32)
        for e in range(2):
            lanes = slice(e * 128, e * 128 + 128)
            k2[part, 32:40, lanes] = row_got[64 + e * 16 + part * 8 : 64 + e * 16 + part * 8 + 8]
            k2[part, 40:44, lanes] = corner_got[8 + e * 8 + part * 4 : 8 + e * 8 + part * 4 + 4]
        k2[part, 44:48] = jnp.zeros((4, nz // 2), F32)
        high, low = split(k2[part])
        grid = later_z_ref[0, nz : nz + 16]
        if part == 1:
            grid = jnp.zeros_like(grid)
        rest = jnp.concatenate([high, low, grid, jnp.zeros((16, nz // 2), BF16)], axis=0)
        t2_ref[part] = t2[part] + dot(later_ref[0:144, cells:], rest)

    for part in range(2):
        rows = jnp.concatenate([row_got[part * 32 + c * 8 : part * 32 + c * 8 + 8] for c in range(nz // 128)], axis=1)
        last = jnp.concatenate([corner_got[part * 4 + c : part * 4 + c + 1] for c in range(nz // 128)], axis=1)
        edge[part] = jnp.concatenate([rows, last, jnp.zeros((7, nz), F32)], axis=0)
    high, low = split(edge[...].reshape(32, nz))
    both = jnp.concatenate([high, low], axis=0)
    gap = jnp.zeros((32, nz // 2), BF16)
    table = first_ref[:, cells:].reshape(3, 3, nx // 2, ny // 2, 128)
    head_ref[...] = table[0:2, :, 0].reshape(-1, 128)
    for a in range(3):
        z = dot(both, z_ref[a, 0:nz])
        zh, zl = split(z[0:32] + z[32:64])
        for part in range(2):
            own = slice(part * 16, part * 16 + 16)
            rest = jnp.concatenate([gap, zh[own], gap, zl[own], gap], axis=0)
            add = dot(table[2, 0:2].reshape(-1, 128), rest).reshape(2, nx // 2, ny // 2, nz // 2)
            one_ref[part, 2, 0:2, a, :, 0:8] += add[:, :, 0:8]
            add = dot(table[0:2, 0:2, 1:].reshape(-1, 128), rest).reshape(2, 2, nx // 2 - 1, ny // 2, nz // 2)
            one_ref[part, 0:2, 0:2, a, 1:, 0:8] += add[:, :, :, 0:8]

    @pl.when(helps)
    def _():
        lead.wait_recv()
        follow.start()

    @pl.when(from_x)
    def _():
        plane_w.wait_recv()
        plane_a.wait_recv()
        x2.wait_recv()

    loads[6].wait()
    for copy in gathers:
        copy.wait_recv()
    for copy in gathers:
        copy.wait_send()
    pl.when(to_y)(row.wait_send)
    pl.when(to_xy)(corner.wait_send)

    pl.when(to_x & jnp.logical_not(leads))(plane_a.wait_send)
    pl.when(leads)(lead.wait_send)
    pl.when(helps)(follow.wait_send)

    @pl.when(to_x)
    def _():
        for copy in (plane_w, x3, x2):
            copy.wait_send()


def result_kernel(
    one_ref, t2_ref, x2_ref, blocks, plane, edge, z_ref, head_ref, gather_ref,
    one_hbm, two_hbm, three_hbm, first, two, three, sem,
):
    nz = plane.shape[2]
    count = one_ref.shape[4]
    copies = [pltpu.make_async_copy(one_ref.at[part, 2], one_hbm.at[part, 2], sem.at[part]) for part in range(2)]
    rest = pl.ds(1, count - 1)
    for part in range(2):
        for a in range(2):
            slot = sem.at[2 + 2 * part + a]
            copies.append(
                pltpu.make_async_copy(one_ref.at[part, a, :, :, rest], one_hbm.at[part, a, :, :, rest], slot)
            )
    for copy in copies:
        copy.start()

    w, a = plane[0], plane[1]
    value = jnp.concatenate([-(w + 0.5 * a), edge[0], 0.5 * w - a, edge[1]], axis=0)
    high, low = split(value)
    both = jnp.concatenate([high, low], axis=0)
    half = 2 * HALO
    for a in range(3):
        z = dot(both, z_ref[a, 0:nz])
        zh, zl = split(z[0:half] + z[half:])
        for part in range(2):
            own = slice(part * HALO, part * HALO + HALO)
            rest = jnp.concatenate([zh[own], zl[own], jnp.zeros((32, nz // 2), BF16)], axis=0)
            add = dot(head_ref[...], rest)
            first[part, :, :, a] = one_ref[part, 0:2, :, a, 0] + add.reshape(2, 3, -1, nz // 2)
    for part in range(2):
        for a in range(2):
            slot = sem.at[6 + 2 * part + a]
            copy = pltpu.make_async_copy(first.at[part, a], one_hbm.at[part, a, :, :, 0], slot)
            copy.start()
            copies.append(copy)

    _, _, _, _, m, n, depth = two.shape
    for part in range(2):
        whole = t2_ref[part].reshape(3, 3, m, n, 2 * depth)
        for a in range(3):
            for b in range(3):
                for x in range(m):
                    value = whole[a, b, x]
                    if x == 0 and a < 2:
                        base = part * 32 + a * 2 * n
                        if b > 0:
                            value = value + x2_ref[base + (b - 1) * n : base + b * n]
                        else:
                            above = pltpu.roll(x2_ref[base + n : base + 2 * n], 1, 0)
                            line = lax.broadcasted_iota(jnp.int32, above.shape, 0)
                            value = value + jnp.where(line == 0, 0.0, above)
                    two[part, a, b, 1, x] = value[:, 0:depth]
                    two[part, a, b, 2, x] = value[:, depth:]
                    two[part, a, b, 0, x] = pltpu.roll(value[:, depth:], 1, 1)
    copies.append(pltpu.make_async_copy(two, two_hbm, sem.at[10]))
    copies[-1].start()

    shape = three.shape[1:3] + three.shape[4:]
    for part in range(2):
        rows = jnp.concatenate([blocks[g, part * 24 : part * 24 + 24] for g in range(blocks.shape[0])], axis=0)
        high, low = split(rows)
        out = dot(gather_ref[...], jnp.concatenate([high, low], axis=0))
        lane = lax.broadcasted_iota(jnp.int32, out.shape, 1)
        upper = pltpu.roll(out, 64, 1)
        lower = jnp.where(lane == 0, 0.0, pltpu.roll(out, 65, 1))
        three[part, :, :, 1] = out[:, 0:64].reshape(shape)
        three[part, :, :, 2] = upper[:, 0:64].reshape(shape)
        three[part, :, :, 0] = lower[:, 0:64].reshape(shape)
    copies.append(pltpu.make_async_copy(three, three_hbm, sem.at[11]))
    copies[-1].start()
    for copy in copies:
        copy.wait()


def solution(mesh):
    sx, sy = mesh.shape["gx"], mesh.shape["gy"]

    def local(wave_sq, absorb):
        nx, ny, nz = wave_sq.shape
        first, later = xy_tables(nx, ny, sx, sy)
        tables = [
            jnp.asarray(t.astype(ml_dtypes.bfloat16)) for t in (first, later, z_tables(nz), gather_table(sy, ny // 8))
        ]
        first, later, depth, gather = tables
        half = nz // 2
        level_one = jax.ShapeDtypeStruct((2, 3, 3, 3, nx // 2, ny // 2, nz // 2), F32)
        level_two = jax.ShapeDtypeStruct((2, 3, 3, 3, nx // 4, ny // 4, nz // 4), F32)
        level_three = jax.ShapeDtypeStruct((2, 3, 3, 3, nx // 8, sy * ny // 8, nz // 8), F32)
        parts = pl.pallas_call(
            functools.partial(halo_kernel, sx, sy),
            out_shape=(
                level_one,
                jax.ShapeDtypeStruct((2, 144, half), F32),
                jax.ShapeDtypeStruct((64, half), F32),
                jax.ShapeDtypeStruct((sy, 48, 128), F32),
                jax.ShapeDtypeStruct((2, ny, nz), F32),
                jax.ShapeDtypeStruct((2, 16, nz), F32),
                jax.ShapeDtypeStruct((3, *depth.shape[1:]), BF16),
                jax.ShapeDtypeStruct((3 * ny, 128), BF16),
                jax.ShapeDtypeStruct(gather.shape, BF16),
            ),
            in_specs=[pl.BlockSpec(memory_space=pltpu.HBM)] * 6,
            out_specs=[pl.BlockSpec(memory_space=pltpu.VMEM)] * 9,
            scratch_shapes=[
                pltpu.VMEM((nx, ny, nz), F32),
                pltpu.VMEM((nx, ny, nz), F32),
                pltpu.VMEM(first.shape[1:], BF16),
                pltpu.VMEM(later.shape[1:], BF16),
                pltpu.VMEM((2, *depth.shape[1:]), BF16),
                pltpu.VMEM((2, 2, nx * ny, nz), BF16),
                pltpu.VMEM((104, 128), F32),
                pltpu.VMEM((104, 128), F32),
                pltpu.VMEM((32, 128), F32),
                pltpu.VMEM((32, 128), F32),
                pltpu.VMEM((64, half), F32),
                pltpu.VMEM((32, 128), F32),
                pltpu.VMEM((32, 128), F32),
                pltpu.VMEM((2, 144, half), F32),
                pltpu.VMEM((2, 32, 128), F32),
                pltpu.VMEM((2, HALO, half), F32),
                pltpu.VMEM((2, 32, 128), F32),
                pltpu.VMEM((2, nz // 128, nx, 128), F32),
                pltpu.VMEM((ny, nz), F32),
                pltpu.SemaphoreType.DMA((7,)),
                pltpu.SemaphoreType.DMA((7 + sy,)),
                pltpu.SemaphoreType.DMA((7 + sy,)),
            ],
            compiler_params=pltpu.CompilerParams(
                collective_id=0, has_side_effects=True, vmem_limit_bytes=32 * 1024 * 1024
            ),
        )(*[pltpu.with_memory_space_constraint(v, pltpu.HBM) for v in (wave_sq, absorb, first, later, depth, gather)])
        return pl.pallas_call(
            result_kernel,
            out_shape=(level_one, level_two, level_three),
            in_specs=[pl.BlockSpec(memory_space=pltpu.VMEM)] * 9,
            out_specs=[pl.BlockSpec(memory_space=pltpu.HBM)] * 3,
            scratch_shapes=[
                pltpu.VMEM((2, 2, 3, 3, ny // 2, half), F32),
                pltpu.VMEM(level_two.shape, F32),
                pltpu.VMEM(level_three.shape, F32),
                pltpu.SemaphoreType.DMA((12,)),
            ],
            compiler_params=pltpu.CompilerParams(vmem_limit_bytes=16 * 1024 * 1024),
        )(*parts)

    return jax.shard_map(
        local,
        mesh=mesh,
        in_specs=(P("gx", "gy", None), P("gx", "gy", None)),
        out_specs=(
            P(None, None, None, None, "gx", "gy", None),
            P(None, None, None, None, "gx", "gy", None),
            P(None, None, None, None, "gx", None, None),
        ),
        check_vma=False,
    )
```

```python
import functools

import jax
import jax.numpy as jnp
import ml_dtypes
import numpy as np
from jax import lax
from jax.experimental import pallas as pl
from jax.experimental.pallas import tpu as pltpu
from jax.sharding import PartitionSpec as P

MESH = pl.DeviceIdType.MESH
BF16 = jnp.bfloat16
F32 = jnp.float32
FIRST, MIDDLE, LAST = 0, 1, 2


def hat(distance, width):
    return np.maximum(0.0, 1.0 - np.abs(distance) / width)


def line_weights(cells, level, place):
    width = 2**level
    coarse = cells // width
    fine = np.arange(cells)[None, :]
    node = width * np.arange(coarse)[:, None]
    table = np.stack([hat(fine - node, width) * hat(fine - node - a * width, width) for a in (-1, 0, 1)])
    table /= width
    if place == LAST:
        table[2, -1] = 0.0
    return table


def tail_weights(cells, level, place):
    width = 2**level
    distance = np.arange(cells) - cells
    table = np.stack([hat(distance, width) * hat(distance + width, width), hat(distance, width) ** 2]) / width
    return table * (place != LAST)


def grid_tables(cells):
    lap = np.zeros((cells, 3))
    lap[:] = (-1.0, 2.0, -1.0)
    lap[0, 0] = lap[-1, 2] = 0.0
    one = np.zeros((cells, 3))
    one[:, 1] = 1.0

    def coarsen(band):
        coarse = band.shape[0] // 2
        out = np.zeros((coarse, 3))
        for row in range(coarse):
            for a in (-1, 0, 1):
                if not 0 <= row + a < coarse:
                    continue
                for step, weight in ((-1, 0.25), (0, 0.5), (1, 0.25)):
                    fine = 2 * row + step
                    if fine < 0:
                        continue
                    for b in (-1, 0, 1):
                        distance = abs(fine + b - 2 * (row + a))
                        spread = 1.0 if distance == 0 else 0.5 if distance == 1 else 0.0
                        out[row, a + 1] += weight * spread * band[fine, b + 1]
        return out

    tables = []
    for _ in range(3):
        lap, one = coarsen(lap), coarsen(one)
        tables.append((lap.T, one.T))
    return tables


def two_terms(table):
    high = table.astype(ml_dtypes.bfloat16).astype(np.float64)
    return high, table - high


def row_features(lap, one):
    (lh, ll), (oh, ol) = two_terms(lap), two_terms(one)
    columns = [lh, lh, ll, ll, oh, oh, ol, ol]
    return np.stack(columns + [np.zeros_like(lh)] * 8, axis=1)


def column_features(lap, one):
    (lh, ll), (oh, ol) = two_terms(lap), two_terms(one)
    rows = [oh, ol, oh, ol, lh, ll, lh, ll]
    return np.stack(rows + [np.zeros_like(lh)] * 8, axis=0)


def place_slice(table, place, cells):
    whole = table.shape[1]
    start = {FIRST: 0, MIDDLE: cells, LAST: whole - cells}[place]
    return table[:, start : start + cells]


def grid_rows(grid_x, grid_y, place_x, place_y, cells_x, cells_y):
    lap_x, one_x = (place_slice(t, place_x, cells_x)[:, None, :, None] for t in grid_x)
    lap_y, one_y = (place_slice(t, place_y, cells_y)[None, :, None, :] for t in grid_y)
    lap = (lap_x * one_y + one_x * lap_y).reshape(-1)
    one = (one_x * one_y).reshape(-1)
    return row_features(lap, one)


def padded(rows, count, width=None):
    out = np.zeros((count, rows.shape[1] if width is None else width))
    out[: rows.shape[0], : rows.shape[1]] = rows
    return out


def pair(left, right):
    both = np.einsum("aJi,bKj->abJKij", left, right)
    return both.reshape(-1, left.shape[2] * right.shape[2])


def xy_tables(nx, ny, sx, sy):
    grid_x, grid_y = grid_tables(nx * sx), grid_tables(ny * sy)
    first, later = [], []
    for px in (FIRST, MIDDLE, LAST):
        for py in (FIRST, MIDDLE, LAST):
            wx = [line_weights(nx, k, px) for k in (1, 2, 3)]
            wy = [line_weights(ny, k, py) for k in (1, 2, 3)]
            tx = [tail_weights(nx, k, px)[:, None, :] for k in (1, 2, 3)]
            ty = [tail_weights(ny, k, py)[:, None, :] for k in (1, 2, 3)]

            own = pair(wx[0], wy[0])
            head_x = np.zeros((3, nx // 2, 1))
            head_x[0:2, 0, 0] = 0.125 * (px != FIRST)
            head_y = np.zeros((3, ny // 2, 1))
            head_y[0:2, 0, 0] = 0.125 * (py != FIRST)
            halo = np.concatenate([pair(head_x, wy[0]), pair(wx[0], head_y), pair(head_x, head_y)], axis=1)
            halo = padded(halo, halo.shape[0], HALO)
            grid = grid_rows(grid_x[0], grid_y[0], px, py, nx // 2, ny // 2)
            first.append(padded(np.concatenate([own, halo, halo, grid], axis=1), own.shape[0], nx * ny + 128))

            m, n = nx // 4, ny // 4
            own = pair(wx[1], wy[1])
            send = [pair(tx[1], wy[1][1:]), pair(wx[1][1:], ty[1]), pair(tx[1], ty[1])]
            rows2 = padded(np.concatenate([own, *send]), 192)
            take = np.zeros((3, 3, m, n, HALO))
            for a in range(2):
                for j in range(n):
                    take[a, 1, 0, j, a * 2 * n + j] = 1.0
                    take[a, 2, 0, j, a * 2 * n + n + j] = 1.0
                    if j + 1 < n:
                        take[a, 0, 0, j + 1, a * 2 * n + n + j] = 1.0
                for i in range(m):
                    own_e, own_f = 4 * n + a * m + i, 4 * n + (2 + a) * m + i
                    take[1, a, i, 0, own_e] = 1.0
                    take[2, a, i, 0, own_f] = 1.0
                    if i + 1 < m:
                        take[0, a, i + 1, 0, own_f] = 1.0
                for b in range(2):
                    take[a, b, 0, 0, 4 * n + 4 * m + 2 * a + b] = 1.0
            take = take.reshape(-1, HALO)
            grid = grid_rows(grid_x[1], grid_y[1], px, py, m, n)
            take2 = np.concatenate([take, take, grid], axis=1)

            n = ny // 8
            own = padded(pair(wx[2], wy[2][1:]), 32)
            send = [pair(tx[2], wy[2][1:]), pair(wx[2][1:], ty[2]), pair(tx[2], ty[2])]
            rows3 = padded(np.concatenate([own, *send]), 64)
            take = np.zeros((3, 2, n, 32))
            for a in range(2):
                for e in range(2):
                    for j in range(n):
                        take[a, e, j, (a * 2 + e) * n + j] = 1.0
                take[1 + a, 0, 0, 4 * n + 2 * a + 1] = 1.0
                take[a, 0, 0, 4 * n + 4 + 2 * a + 1] = 1.0
            take = take.reshape(-1, 32)
            grid = grid_rows(grid_x[2], grid_y[2], px, py, 1, n).reshape(3, 3, n, 16)[:, 1:].reshape(-1, 16)
            take3 = np.concatenate([take, take, grid], axis=1)

            table = np.zeros((320, nx * ny + 128))
            high, low = two_terms(rows3)
            table[:, : nx * ny] = np.concatenate([rows2, high, low])
            table[: take2.shape[0], nx * ny : nx * ny + take2.shape[1]] = take2
            table[192 : 192 + take3.shape[0], nx * ny : nx * ny + take3.shape[1]] = take3
            later.append(table)
    return np.stack(first), np.stack(later)


def z_tables(nz):
    grid = grid_tables(nz)
    half = nz // 2
    blocks = []
    one = line_weights(nz, 1, LAST)
    one[0, 0] = 0.0
    for a in range(3):
        blocks.append(np.concatenate([one[a].T, column_features(grid[0][0][a], grid[0][1][a])]))
    for k in (2, 3):
        table = line_weights(nz, k, LAST)
        columns = [
            np.concatenate([table[a].T, column_features(grid[k - 1][0][a], grid[k - 1][1][a])]) for a in (1, 2)
        ]
        block = np.concatenate(columns, axis=1)
        blocks.append(padded(block, nz + 16, half))
    return np.stack(blocks)


def gather_table(parts, n):
    table = np.zeros((3, 3, parts * n, parts, 3, 2, n))
    for a in range(3):
        for g in range(parts):
            for j in range(n):
                row = g * n + j
                table[a, 1, row, g, a, 0, j] = 1.0
                table[a, 2, row, g, a, 1, j] = 1.0
                if row + 1 < parts * n:
                    table[a, 0, row + 1, g, a, 1, j] = 1.0
    table = table.reshape(9 * parts * n, -1)
    return np.concatenate([table, table], axis=1)


HALO = 48
TURNS = 4
RELAYS = (7, 3)


def split(value):
    high = value.astype(BF16)
    return high, (value - high.astype(F32)).astype(BF16)


def dot(left, right):
    return jnp.dot(left, right, preferred_element_type=F32)


def exact_dot(left, value):
    high, low = split(value)
    return dot(left, high) + dot(left, low)


def halo_kernel(
    sx, sy,
    w_hbm, a_hbm, first_hbm, later_hbm, z_hbm, gather_hbm,
    one_ref, t2_ref, x2_got, blocks, plane, edge, z_ref, head_ref, gather_ref,
    w_ref, a_ref, first_ref, later_ref, later_z_ref,
    mass, row_send, row_got, corner_send, corner_got,
    x2_send, x3_send, x3_got, t2, t3, k2, k3, raw, through,
    load_sem, send_sem, got_sem,
):
    ix, iy = lax.axis_index("gx"), lax.axis_index("gy")
    nx, ny, nz = w_hbm.shape
    cells = nx * ny
    next_x, last_x = lax.rem(ix + 1, sx), lax.rem(ix + sx - 1, sx)
    next_y, last_y = lax.rem(iy + 1, sy), lax.rem(iy + sy - 1, sy)
    from_x, to_x, from_y, to_y = ix > 0, ix < sx - 1, iy > 0, iy < sy - 1
    from_xy, to_xy = from_x & from_y, to_x & to_y
    turn = sx // TURNS
    turning = sx == TURNS * 32
    at = lax.rem(ix, turn)
    leads = to_x & (at == turn - 1) & turning
    helps = [(ix < sx - turn) & (at == place) & turning for place in RELAYS]
    waits = from_x & (at == 0) & turning
    upper = iy >= sy // 2
    yields = to_x & turning & (((at == turn - 2) & upper) | ((at == turn - 4) & jnp.logical_not(upper)))
    peers = [lax.rem(iy + step, sy) for step in range(1, sy)]

    place_x = jnp.where(ix == 0, FIRST, jnp.where(ix == sx - 1, LAST, MIDDLE))
    place_y = jnp.where(iy == 0, FIRST, jnp.where(iy == sy - 1, LAST, MIDDLE))
    place = place_x * 3 + place_y
    loads = [
        pltpu.make_async_copy(src, dst, load_sem.at[i])
        for i, (src, dst) in enumerate(
            (
                (w_hbm, w_ref),
                (a_hbm, a_ref),
                (later_hbm.at[place], later_ref),
                (z_hbm.at[pl.ds(3, 2)], later_z_ref),
                (z_hbm.at[pl.ds(0, 3)], z_ref),
                (first_hbm.at[place], first_ref),
                (gather_hbm, gather_ref),
            )
        )
    ]
    for load in loads[:4]:
        load.start()

    @pl.when(jnp.logical_not(from_x))
    def _():
        plane[...] = jnp.zeros_like(plane)
        x2_got[...] = jnp.zeros_like(x2_got)
        x3_got[...] = jnp.zeros_like(x3_got)

    @pl.when(jnp.logical_not(from_y))
    def _():
        row_got[...] = jnp.zeros_like(row_got)

    @pl.when(jnp.logical_not(from_xy))
    def _():
        corner_got[...] = jnp.zeros_like(corner_got)

    def signal(*device):
        pl.semaphore_signal(barrier, inc=1, device_id=device, device_id_type=MESH)

    barrier = pltpu.get_barrier_semaphore()
    for p in peers:
        signal(ix, p)
    pl.when(from_x)(lambda: signal(last_x, iy))
    pl.when(from_xy)(lambda: signal(last_x, last_y))
    for i, place in enumerate(RELAYS):
        pl.when(waits)(lambda place=place: signal(ix - turn + place, iy))
        pl.when(helps[i])(lambda place=place: signal(ix + turn - 1 - place, iy))
    sends_to = [flag.astype(jnp.int32) for flag in (to_x, to_xy, leads, leads, *helps)]
    pl.semaphore_wait(barrier, sy - 1 + sum(sends_to))

    def remote(slot, src, dst, device, got=None):
        got = slot if got is None else got
        return pltpu.make_async_remote_copy(
            src_ref=src, dst_ref=dst, send_sem=send_sem.at[slot], recv_sem=got_sem.at[got],
            device_id=device, device_id_type=MESH,
        )

    plane_w = remote(0, w_hbm.at[nx - 1], plane.at[0], (next_x, iy))
    plane_a = remote(1, a_hbm.at[nx - 1], plane.at[1], (next_x, iy))
    x3 = remote(2, x3_send, x3_got, (next_x, iy))
    x2 = remote(3, x2_send, x2_got, (next_x, iy))
    row = remote(4, row_send, row_got, (ix, next_y))
    corner = remote(5, corner_send, corner_got, (next_x, next_y))
    gathers = [remote(6 + i, blocks.at[iy], blocks.at[iy], (ix, p)) for i, p in enumerate(peers)]

    leading, follows = [], []
    for i, place in enumerate(RELAYS):
        source = (w_hbm, a_hbm)[i].at[nx - 1]
        first_stop = jnp.maximum(ix - turn + 1 + place, 0)
        goal = jnp.minimum(ix + turn - place, sx - 1)
        leading.append(remote(5 + sy + i, source, through, (first_stop, iy)))
        follows.append(remote(7 + sy + i, through, plane.at[i], (goal, iy), got=i))

    pl.when(to_x & jnp.logical_not(leads | yields))(plane_w.start)

    @pl.when(leads)
    def _():
        for copy in leading:
            copy.start()

    for load in loads[4:]:
        load.start()

    loads[0].wait()
    loads[1].wait()
    for x in range(nx):
        w, a = w_ref[x], a_ref[x]
        for part, value in enumerate((-(w + 0.5 * a), 0.5 * w - a)):
            high, low = split(value)
            mass[part, 0, x * ny : (x + 1) * ny] = high
            mass[part, 1, x * ny : (x + 1) * ny] = low
            for c in range(nz // 128):
                raw[part, c, x : x + 1] = value[ny - 1 : ny, c * 128 : (c + 1) * 128]
    loads[2].wait()
    loads[3].wait()

    for part in range(2):
        table = later_ref[:, 0:cells]
        rows = dot(table, mass[part, 0]) + dot(table, mass[part, 1])
        high, low = split(rows[0:192])
        two = dot(high, later_z_ref[0, 0:nz]) + dot(low, later_z_ref[0, 0:nz])
        high, low = split(rows[192:256] + rows[256:320])
        three = dot(high, later_z_ref[1, 0:nz, 0:128]) + dot(low, later_z_ref[1, 0:nz, 0:128])
        t2[part] = two[0:144]
        t3[part] = three[0:32]
        x3_send[part * 16 : part * 16 + 16] = three[32:48]
        x2_send[part * 32 : part * 32 + 32] = two[144:176]
        for e in range(2):
            row_send[64 + e * 16 + part * 8 : 64 + e * 16 + part * 8 + 8] = two[176:184, e * 128 : e * 128 + 128]
            corner_send[8 + e * 8 + part * 4 : 8 + e * 8 + part * 4 + 4] = two[184:188, e * 128 : e * 128 + 128]
        row_send[96 + part * 4 : 96 + part * 4 + 4] = three[48:52]
        corner_send[24 + part * 4 : 24 + part * 4 + 4] = three[52:56]
        for c in range(nz // 128):
            row_send[part * 32 + c * 8 : part * 32 + c * 8 + 8] = raw[part, c]
            corner_send[part * 4 + c : part * 4 + c + 1] = raw[part, c, nx - 1 : nx]

    pl.when(to_x)(x3.start)
    pl.when(to_xy)(corner.start)
    pl.when(to_y & jnp.logical_not(leads))(row.start)

    pl.when(to_x & jnp.logical_not(leads | yields))(plane_a.start)
    pl.when(to_x)(x2.start)
    pl.when(to_y & leads)(row.start)

    loads[4].wait()
    loads[5].wait()

    def own_level_one(i, carry):
        part, a = i // 3, lax.rem(i, 3)
        table = z_ref[a]
        z = dot(mass[part, 0], table[0:nz]) + dot(mass[part, 1], table[0:nz])
        high, low = split(z)
        grid = jnp.where(part == 0, table[nz : nz + 16], jnp.zeros((16, nz // 2), BF16))
        rest = jnp.concatenate([jnp.zeros((2 * HALO, nz // 2), BF16), grid, jnp.zeros((16, nz // 2), BF16)], axis=0)
        for ax in range(3):
            rows = first_ref[ax * 192 : ax * 192 + 192]
            out = dot(rows[:, 0:cells], high) + dot(rows[:, 0:cells], low) + dot(rows[:, cells:], rest)
            one_ref[part, ax, :, a] = out.reshape(3, nx // 2, ny // 2, nz // 2)
        return carry

    lax.fori_loop(0, 6, own_level_one, 0)

    @pl.when(yields)
    def _():
        plane_w.start()
        plane_a.start()

    pl.when(from_y)(row.wait_recv)
    for part in range(2):
        rows = jnp.concatenate([row_got[part * 32 + c * 8 : part * 32 + c * 8 + 8] for c in range(nz // 128)], axis=1)
        edge[part] = jnp.concatenate([rows, jnp.zeros((8, nz), F32)], axis=0)
    high, low = split(edge[...].reshape(32, nz))
    both = jnp.concatenate([high, low], axis=0)
    gap = jnp.zeros((32, nz // 2), BF16)
    table = first_ref[:, cells:].reshape(3, 3, nx // 2, ny // 2, 128)
    head_ref[...] = table[0:2, :, 0].reshape(-1, 128)
    for a in range(3):
        z = dot(both, z_ref[a, 0:nz])
        zh, zl = split(z[0:32] + z[32:64])
        for part in range(2):
            own = slice(part * 16, part * 16 + 16)
            rest = jnp.concatenate([gap, zh[own], gap, zl[own], gap], axis=0)
            add = dot(table[2, 0:2].reshape(-1, 128), rest).reshape(2, nx // 2, ny // 2, nz // 2)
            one_ref[part, 2, 0:2, a, :, 0:8] += add[:, :, 0:8]
            add = dot(table[0:2, 0:2, 1:].reshape(-1, 128), rest).reshape(2, 2, nx // 2 - 1, ny // 2, nz // 2)
            one_ref[part, 0:2, 0:2, a, 1:, 0:8] += add[:, :, :, 0:8]

    pl.when(from_xy)(corner.wait_recv)
    pl.when(from_x)(x3.wait_recv)
    for part in range(2):
        k3[part, 0:16] = x3_got[part * 16 : part * 16 + 16]
        k3[part, 16:20] = row_got[96 + part * 4 : 96 + part * 4 + 4]
        k3[part, 20:24] = corner_got[24 + part * 4 : 24 + part * 4 + 4]
        k3[part, 24:32] = jnp.zeros((8, 128), F32)
        high, low = split(k3[part])
        grid = later_z_ref[1, nz : nz + 16, 0:128]
        if part == 1:
            grid = jnp.zeros_like(grid)
        rest = jnp.concatenate([high, low, grid, jnp.zeros((48, 128), BF16)], axis=0)
        own = t3[part] + dot(later_ref[192:224, cells:], rest)
        blocks[iy, part * 24 : part * 24 + 24] = own[0:24]
    for copy in gathers:
        copy.start()

    for part in range(2):
        edge[part, 8:9] = jnp.concatenate([corner_got[part * 4 + c : part * 4 + c + 1] for c in range(nz // 128)], axis=1)

    for part in range(2):
        k2[part, 0:32] = jnp.zeros((32, nz // 2), F32)
        for e in range(2):
            lanes = slice(e * 128, e * 128 + 128)
            k2[part, 32:40, lanes] = row_got[64 + e * 16 + part * 8 : 64 + e * 16 + part * 8 + 8]
            k2[part, 40:44, lanes] = corner_got[8 + e * 8 + part * 4 : 8 + e * 8 + part * 4 + 4]
        k2[part, 44:48] = jnp.zeros((4, nz // 2), F32)
        high, low = split(k2[part])
        grid = later_z_ref[0, nz : nz + 16]
        if part == 1:
            grid = jnp.zeros_like(grid)
        rest = jnp.concatenate([high, low, grid, jnp.zeros((16, nz // 2), BF16)], axis=0)
        t2_ref[part] = t2[part] + dot(later_ref[0:144, cells:], rest)

    for i in range(2):

        @pl.when(helps[i])
        def _(i=i):
            leading[i].wait_recv()
            follows[i].start()

    @pl.when(from_x)
    def _():
        plane_w.wait_recv()
        plane_a.wait_recv()
        x2.wait_recv()

    loads[6].wait()
    for copy in gathers:
        copy.wait_recv()
    for copy in gathers:
        copy.wait_send()
    pl.when(to_y)(row.wait_send)
    pl.when(to_xy)(corner.wait_send)


    @pl.when(to_x & jnp.logical_not(leads))
    def _():
        plane_w.wait_send()
        plane_a.wait_send()

    @pl.when(leads)
    def _():
        for copy in leading:
            copy.wait_send()

    for i in range(2):
        pl.when(helps[i])(follows[i].wait_send)

    @pl.when(to_x)
    def _():
        x3.wait_send()
        x2.wait_send()


def result_kernel(
    one_ref, t2_ref, x2_ref, blocks, plane, edge, z_ref, head_ref, gather_ref,
    one_hbm, two_hbm, three_hbm, first, two, three, sem,
):
    nz = plane.shape[2]
    count = one_ref.shape[4]
    copies = [pltpu.make_async_copy(one_ref.at[part, 2], one_hbm.at[part, 2], sem.at[part]) for part in range(2)]
    rest = pl.ds(1, count - 1)
    for part in range(2):
        for a in range(2):
            slot = sem.at[2 + 2 * part + a]
            copies.append(
                pltpu.make_async_copy(one_ref.at[part, a, :, :, rest], one_hbm.at[part, a, :, :, rest], slot)
            )
    for copy in copies:
        copy.start()

    w, a = plane[0], plane[1]
    value = jnp.concatenate([-(w + 0.5 * a), edge[0], 0.5 * w - a, edge[1]], axis=0)
    high, low = split(value)
    both = jnp.concatenate([high, low], axis=0)
    half = 2 * HALO
    for a in range(3):
        z = dot(both, z_ref[a, 0:nz])
        zh, zl = split(z[0:half] + z[half:])
        for part in range(2):
            own = slice(part * HALO, part * HALO + HALO)
            rest = jnp.concatenate([zh[own], zl[own], jnp.zeros((32, nz // 2), BF16)], axis=0)
            add = dot(head_ref[...], rest)
            first[part, :, :, a] = one_ref[part, 0:2, :, a, 0] + add.reshape(2, 3, -1, nz // 2)
    for part in range(2):
        for a in range(2):
            slot = sem.at[6 + 2 * part + a]
            copy = pltpu.make_async_copy(first.at[part, a], one_hbm.at[part, a, :, :, 0], slot)
            copy.start()
            copies.append(copy)

    _, _, _, _, m, n, depth = two.shape
    for part in range(2):
        whole = t2_ref[part].reshape(3, 3, m, n, 2 * depth)
        for a in range(3):
            for b in range(3):
                for x in range(m):
                    value = whole[a, b, x]
                    if x == 0 and a < 2:
                        base = part * 32 + a * 2 * n
                        if b > 0:
                            value = value + x2_ref[base + (b - 1) * n : base + b * n]
                        else:
                            above = pltpu.roll(x2_ref[base + n : base + 2 * n], 1, 0)
                            line = lax.broadcasted_iota(jnp.int32, above.shape, 0)
                            value = value + jnp.where(line == 0, 0.0, above)
                    two[part, a, b, 1, x] = value[:, 0:depth]
                    two[part, a, b, 2, x] = value[:, depth:]
                    two[part, a, b, 0, x] = pltpu.roll(value[:, depth:], 1, 1)
    copies.append(pltpu.make_async_copy(two, two_hbm, sem.at[10]))
    copies[-1].start()

    shape = three.shape[1:3] + three.shape[4:]
    for part in range(2):
        rows = jnp.concatenate([blocks[g, part * 24 : part * 24 + 24] for g in range(blocks.shape[0])], axis=0)
        high, low = split(rows)
        out = dot(gather_ref[...], jnp.concatenate([high, low], axis=0))
        lane = lax.broadcasted_iota(jnp.int32, out.shape, 1)
        upper = pltpu.roll(out, 64, 1)
        lower = jnp.where(lane == 0, 0.0, pltpu.roll(out, 65, 1))
        three[part, :, :, 1] = out[:, 0:64].reshape(shape)
        three[part, :, :, 2] = upper[:, 0:64].reshape(shape)
        three[part, :, :, 0] = lower[:, 0:64].reshape(shape)
    copies.append(pltpu.make_async_copy(three, three_hbm, sem.at[11]))
    copies[-1].start()
    for copy in copies:
        copy.wait()


def solution(mesh):
    sx, sy = mesh.shape["gx"], mesh.shape["gy"]

    def local(wave_sq, absorb):
        nx, ny, nz = wave_sq.shape
        first, later = xy_tables(nx, ny, sx, sy)
        tables = [
            jnp.asarray(t.astype(ml_dtypes.bfloat16)) for t in (first, later, z_tables(nz), gather_table(sy, ny // 8))
        ]
        first, later, depth, gather = tables
        half = nz // 2
        level_one = jax.ShapeDtypeStruct((2, 3, 3, 3, nx // 2, ny // 2, nz // 2), F32)
        level_two = jax.ShapeDtypeStruct((2, 3, 3, 3, nx // 4, ny // 4, nz // 4), F32)
        level_three = jax.ShapeDtypeStruct((2, 3, 3, 3, nx // 8, sy * ny // 8, nz // 8), F32)
        parts = pl.pallas_call(
            functools.partial(halo_kernel, sx, sy),
            out_shape=(
                level_one,
                jax.ShapeDtypeStruct((2, 144, half), F32),
                jax.ShapeDtypeStruct((64, half), F32),
                jax.ShapeDtypeStruct((sy, 48, 128), F32),
                jax.ShapeDtypeStruct((2, ny, nz), F32),
                jax.ShapeDtypeStruct((2, 16, nz), F32),
                jax.ShapeDtypeStruct((3, *depth.shape[1:]), BF16),
                jax.ShapeDtypeStruct((3 * ny, 128), BF16),
                jax.ShapeDtypeStruct(gather.shape, BF16),
            ),
            in_specs=[pl.BlockSpec(memory_space=pltpu.HBM)] * 6,
            out_specs=[pl.BlockSpec(memory_space=pltpu.VMEM)] * 9,
            scratch_shapes=[
                pltpu.VMEM((nx, ny, nz), F32),
                pltpu.VMEM((nx, ny, nz), F32),
                pltpu.VMEM(first.shape[1:], BF16),
                pltpu.VMEM(later.shape[1:], BF16),
                pltpu.VMEM((2, *depth.shape[1:]), BF16),
                pltpu.VMEM((2, 2, nx * ny, nz), BF16),
                pltpu.VMEM((104, 128), F32),
                pltpu.VMEM((104, 128), F32),
                pltpu.VMEM((32, 128), F32),
                pltpu.VMEM((32, 128), F32),
                pltpu.VMEM((64, half), F32),
                pltpu.VMEM((32, 128), F32),
                pltpu.VMEM((32, 128), F32),
                pltpu.VMEM((2, 144, half), F32),
                pltpu.VMEM((2, 32, 128), F32),
                pltpu.VMEM((2, HALO, half), F32),
                pltpu.VMEM((2, 32, 128), F32),
                pltpu.VMEM((2, nz // 128, nx, 128), F32),
                pltpu.VMEM((ny, nz), F32),
                pltpu.SemaphoreType.DMA((7,)),
                pltpu.SemaphoreType.DMA((9 + sy,)),
                pltpu.SemaphoreType.DMA((9 + sy,)),
            ],
            compiler_params=pltpu.CompilerParams(
                collective_id=0, has_side_effects=True, vmem_limit_bytes=32 * 1024 * 1024
            ),
        )(*[pltpu.with_memory_space_constraint(v, pltpu.HBM) for v in (wave_sq, absorb, first, later, depth, gather)])
        return pl.pallas_call(
            result_kernel,
            out_shape=(level_one, level_two, level_three),
            in_specs=[pl.BlockSpec(memory_space=pltpu.VMEM)] * 9,
            out_specs=[pl.BlockSpec(memory_space=pltpu.HBM)] * 3,
            scratch_shapes=[
                pltpu.VMEM((2, 2, 3, 3, ny // 2, half), F32),
                pltpu.VMEM(level_two.shape, F32),
                pltpu.VMEM(level_three.shape, F32),
                pltpu.SemaphoreType.DMA((12,)),
            ],
            compiler_params=pltpu.CompilerParams(vmem_limit_bytes=16 * 1024 * 1024),
        )(*parts)

    return jax.shard_map(
        local,
        mesh=mesh,
        in_specs=(P("gx", "gy", None), P("gx", "gy", None)),
        out_specs=(
            P(None, None, None, None, "gx", "gy", None),
            P(None, None, None, None, "gx", "gy", None),
            P(None, None, None, None, "gx", None, None),
        ),
        check_vma=False,
    )
```

```python
import functools

import jax
import jax.numpy as jnp
import ml_dtypes
import numpy as np
from jax import lax
from jax.experimental import pallas as pl
from jax.experimental.pallas import tpu as pltpu
from jax.sharding import PartitionSpec as P

MESH = pl.DeviceIdType.MESH
BF16 = jnp.bfloat16
F32 = jnp.float32
FIRST, MIDDLE, LAST = 0, 1, 2


def hat(distance, width):
    return np.maximum(0.0, 1.0 - np.abs(distance) / width)


def line_weights(cells, level, place):
    width = 2**level
    coarse = cells // width
    fine = np.arange(cells)[None, :]
    node = width * np.arange(coarse)[:, None]
    table = np.stack([hat(fine - node, width) * hat(fine - node - a * width, width) for a in (-1, 0, 1)])
    table /= width
    if place == LAST:
        table[2, -1] = 0.0
    return table


def tail_weights(cells, level, place):
    width = 2**level
    distance = np.arange(cells) - cells
    table = np.stack([hat(distance, width) * hat(distance + width, width), hat(distance, width) ** 2]) / width
    return table * (place != LAST)


def grid_tables(cells):
    lap = np.zeros((cells, 3))
    lap[:] = (-1.0, 2.0, -1.0)
    lap[0, 0] = lap[-1, 2] = 0.0
    one = np.zeros((cells, 3))
    one[:, 1] = 1.0

    def coarsen(band):
        coarse = band.shape[0] // 2
        out = np.zeros((coarse, 3))
        for row in range(coarse):
            for a in (-1, 0, 1):
                if not 0 <= row + a < coarse:
                    continue
                for step, weight in ((-1, 0.25), (0, 0.5), (1, 0.25)):
                    fine = 2 * row + step
                    if fine < 0:
                        continue
                    for b in (-1, 0, 1):
                        distance = abs(fine + b - 2 * (row + a))
                        spread = 1.0 if distance == 0 else 0.5 if distance == 1 else 0.0
                        out[row, a + 1] += weight * spread * band[fine, b + 1]
        return out

    tables = []
    for _ in range(3):
        lap, one = coarsen(lap), coarsen(one)
        tables.append((lap.T, one.T))
    return tables


def two_terms(table):
    high = table.astype(ml_dtypes.bfloat16).astype(np.float64)
    return high, table - high


def row_features(lap, one):
    (lh, ll), (oh, ol) = two_terms(lap), two_terms(one)
    columns = [lh, lh, ll, ll, oh, oh, ol, ol]
    return np.stack(columns + [np.zeros_like(lh)] * 8, axis=1)


def column_features(lap, one):
    (lh, ll), (oh, ol) = two_terms(lap), two_terms(one)
    rows = [oh, ol, oh, ol, lh, ll, lh, ll]
    return np.stack(rows + [np.zeros_like(lh)] * 8, axis=0)


def place_slice(table, place, cells):
    whole = table.shape[1]
    start = {FIRST: 0, MIDDLE: cells, LAST: whole - cells}[place]
    return table[:, start : start + cells]


def grid_rows(grid_x, grid_y, place_x, place_y, cells_x, cells_y):
    lap_x, one_x = (place_slice(t, place_x, cells_x)[:, None, :, None] for t in grid_x)
    lap_y, one_y = (place_slice(t, place_y, cells_y)[None, :, None, :] for t in grid_y)
    lap = (lap_x * one_y + one_x * lap_y).reshape(-1)
    one = (one_x * one_y).reshape(-1)
    return row_features(lap, one)


def padded(rows, count, width=None):
    out = np.zeros((count, rows.shape[1] if width is None else width))
    out[: rows.shape[0], : rows.shape[1]] = rows
    return out


def pair(left, right):
    both = np.einsum("aJi,bKj->abJKij", left, right)
    return both.reshape(-1, left.shape[2] * right.shape[2])


def xy_tables(nx, ny, sx, sy):
    grid_x, grid_y = grid_tables(nx * sx), grid_tables(ny * sy)
    first, later = [], []
    for px in (FIRST, MIDDLE, LAST):
        for py in (FIRST, MIDDLE, LAST):
            wx = [line_weights(nx, k, px) for k in (1, 2, 3)]
            wy = [line_weights(ny, k, py) for k in (1, 2, 3)]
            tx = [tail_weights(nx, k, px)[:, None, :] for k in (1, 2, 3)]
            ty = [tail_weights(ny, k, py)[:, None, :] for k in (1, 2, 3)]

            own = pair(wx[0], wy[0])
            head_x = np.zeros((3, nx // 2, 1))
            head_x[0:2, 0, 0] = 0.125 * (px != FIRST)
            head_y = np.zeros((3, ny // 2, 1))
            head_y[0:2, 0, 0] = 0.125 * (py != FIRST)
            halo = np.concatenate([pair(head_x, wy[0]), pair(wx[0], head_y), pair(head_x, head_y)], axis=1)
            halo = padded(halo, halo.shape[0], HALO)
            grid = grid_rows(grid_x[0], grid_y[0], px, py, nx // 2, ny // 2)
            first.append(padded(np.concatenate([own, halo, halo, grid], axis=1), own.shape[0], nx * ny + 128))

            m, n = nx // 4, ny // 4
            own = pair(wx[1], wy[1])
            send = [pair(tx[1], wy[1][1:]), pair(wx[1][1:], ty[1]), pair(tx[1], ty[1])]
            rows2 = padded(np.concatenate([own, *send]), 192)
            take = np.zeros((3, 3, m, n, HALO))
            for a in range(2):
                for j in range(n):
                    take[a, 1, 0, j, a * 2 * n + j] = 1.0
                    take[a, 2, 0, j, a * 2 * n + n + j] = 1.0
                    if j + 1 < n:
                        take[a, 0, 0, j + 1, a * 2 * n + n + j] = 1.0
                for i in range(m):
                    own_e, own_f = 4 * n + a * m + i, 4 * n + (2 + a) * m + i
                    take[1, a, i, 0, own_e] = 1.0
                    take[2, a, i, 0, own_f] = 1.0
                    if i + 1 < m:
                        take[0, a, i + 1, 0, own_f] = 1.0
                for b in range(2):
                    take[a, b, 0, 0, 4 * n + 4 * m + 2 * a + b] = 1.0
            take = take.reshape(-1, HALO)
            grid = grid_rows(grid_x[1], grid_y[1], px, py, m, n)
            take2 = np.concatenate([take, take, grid], axis=1)

            n = ny // 8
            own = padded(pair(wx[2], wy[2][1:]), 32)
            send = [pair(tx[2], wy[2][1:]), pair(wx[2][1:], ty[2]), pair(tx[2], ty[2])]
            rows3 = padded(np.concatenate([own, *send]), 64)
            take = np.zeros((3, 2, n, 32))
            for a in range(2):
                for e in range(2):
                    for j in range(n):
                        take[a, e, j, (a * 2 + e) * n + j] = 1.0
                take[1 + a, 0, 0, 4 * n + 2 * a + 1] = 1.0
                take[a, 0, 0, 4 * n + 4 + 2 * a + 1] = 1.0
            take = take.reshape(-1, 32)
            grid = grid_rows(grid_x[2], grid_y[2], px, py, 1, n).reshape(3, 3, n, 16)[:, 1:].reshape(-1, 16)
            take3 = np.concatenate([take, take, grid], axis=1)

            table = np.zeros((320, nx * ny + 128))
            high, low = two_terms(rows3)
            table[:, : nx * ny] = np.concatenate([rows2, high, low])
            table[: take2.shape[0], nx * ny : nx * ny + take2.shape[1]] = take2
            table[192 : 192 + take3.shape[0], nx * ny : nx * ny + take3.shape[1]] = take3
            later.append(table)
    return np.stack(first), np.stack(later)


def z_tables(nz):
    grid = grid_tables(nz)
    half = nz // 2
    blocks = []
    one = line_weights(nz, 1, LAST)
    one[0, 0] = 0.0
    for a in range(3):
        blocks.append(np.concatenate([one[a].T, column_features(grid[0][0][a], grid[0][1][a])]))
    for k in (2, 3):
        table = line_weights(nz, k, LAST)
        columns = [
            np.concatenate([table[a].T, column_features(grid[k - 1][0][a], grid[k - 1][1][a])]) for a in (1, 2)
        ]
        block = np.concatenate(columns, axis=1)
        blocks.append(padded(block, nz + 16, half))
    return np.stack(blocks)


def gather_table(parts, n):
    table = np.zeros((3, 3, parts * n, parts, 3, 2, n))
    for a in range(3):
        for g in range(parts):
            for j in range(n):
                row = g * n + j
                table[a, 1, row, g, a, 0, j] = 1.0
                table[a, 2, row, g, a, 1, j] = 1.0
                if row + 1 < parts * n:
                    table[a, 0, row + 1, g, a, 1, j] = 1.0
    table = table.reshape(9 * parts * n, -1)
    return np.concatenate([table, table], axis=1)


HALO = 48
TURNS = 4
RELAYS = (7, 3)


def split(value):
    high = value.astype(BF16)
    return high, (value - high.astype(F32)).astype(BF16)


def dot(left, right):
    return jnp.dot(left, right, preferred_element_type=F32)


def exact_dot(left, value):
    high, low = split(value)
    return dot(left, high) + dot(left, low)


def halo_kernel(
    sx, sy,
    w_hbm, a_hbm, first_hbm, later_hbm, z_hbm, gather_hbm,
    one_ref, t2_ref, x2_got, blocks, plane, edge, z_ref, head_ref, gather_ref,
    w_ref, a_ref, first_ref, later_ref, later_z_ref,
    mass, row_send, row_got, corner_send, corner_got,
    x2_send, x3_send, x3_got, t2, t3, k2, k3, raw, through,
    load_sem, send_sem, got_sem,
):
    ix, iy = lax.axis_index("gx"), lax.axis_index("gy")
    nx, ny, nz = w_hbm.shape
    cells = nx * ny
    next_x, last_x = lax.rem(ix + 1, sx), lax.rem(ix + sx - 1, sx)
    next_y, last_y = lax.rem(iy + 1, sy), lax.rem(iy + sy - 1, sy)
    from_x, to_x, from_y, to_y = ix > 0, ix < sx - 1, iy > 0, iy < sy - 1
    from_xy, to_xy = from_x & from_y, to_x & to_y
    turn = sx // TURNS
    turning = sx == TURNS * 32
    at = lax.rem(ix, turn)
    leads = to_x & (at == turn - 1) & turning
    helps = [(ix < sx - turn) & (at == place) & turning for place in RELAYS]
    waits = from_x & (at == 0) & turning
    upper = iy >= sy // 2
    yields = to_x & turning & (((at == turn - 2) & upper) | ((at == turn - 4) & jnp.logical_not(upper)))
    peers = [lax.rem(iy + step, sy) for step in range(1, sy)]

    place_x = jnp.where(ix == 0, FIRST, jnp.where(ix == sx - 1, LAST, MIDDLE))
    place_y = jnp.where(iy == 0, FIRST, jnp.where(iy == sy - 1, LAST, MIDDLE))
    place = place_x * 3 + place_y
    loads = [
        pltpu.make_async_copy(src, dst, load_sem.at[i])
        for i, (src, dst) in enumerate(
            (
                (w_hbm, w_ref),
                (a_hbm, a_ref),
                (later_hbm.at[place], later_ref),
                (z_hbm.at[pl.ds(3, 2)], later_z_ref),
                (z_hbm.at[pl.ds(0, 3)], z_ref),
                (first_hbm.at[place], first_ref),
                (gather_hbm, gather_ref),
            )
        )
    ]
    for load in loads[:4]:
        load.start()

    @pl.when(jnp.logical_not(from_x))
    def _():
        plane[...] = jnp.zeros_like(plane)
        x2_got[...] = jnp.zeros_like(x2_got)
        x3_got[...] = jnp.zeros_like(x3_got)

    @pl.when(jnp.logical_not(from_y))
    def _():
        row_got[...] = jnp.zeros_like(row_got)

    @pl.when(jnp.logical_not(from_xy))
    def _():
        corner_got[...] = jnp.zeros_like(corner_got)

    def signal(*device):
        pl.semaphore_signal(barrier, inc=1, device_id=device, device_id_type=MESH)

    barrier = pltpu.get_barrier_semaphore()
    for p in peers:
        signal(ix, p)
    pl.when(from_x)(lambda: signal(last_x, iy))
    pl.when(from_xy)(lambda: signal(last_x, last_y))
    for i, place in enumerate(RELAYS):
        pl.when(waits)(lambda place=place: signal(ix - turn + place, iy))
        pl.when(helps[i])(lambda place=place: signal(ix + turn - 1 - place, iy))
    sends_to = [flag.astype(jnp.int32) for flag in (to_x, to_xy, leads, leads, *helps)]
    pl.semaphore_wait(barrier, sy - 1 + sum(sends_to))

    def remote(slot, src, dst, device, got=None):
        got = slot if got is None else got
        return pltpu.make_async_remote_copy(
            src_ref=src, dst_ref=dst, send_sem=send_sem.at[slot], recv_sem=got_sem.at[got],
            device_id=device, device_id_type=MESH,
        )

    plane_w = remote(0, w_hbm.at[nx - 1], plane.at[0], (next_x, iy))
    plane_a = remote(1, a_hbm.at[nx - 1], plane.at[1], (next_x, iy))
    x3 = remote(2, x3_send, x3_got, (next_x, iy))
    x2 = remote(3, x2_send, x2_got, (next_x, iy))
    row = remote(4, row_send, row_got, (ix, next_y))
    corner = remote(5, corner_send, corner_got, (next_x, next_y))
    gathers = [remote(6 + i, blocks.at[iy], blocks.at[iy], (ix, p)) for i, p in enumerate(peers)]

    leading, follows = [], []
    for i, place in enumerate(RELAYS):
        source = (w_hbm, a_hbm)[i].at[nx - 1]
        first_stop = jnp.maximum(ix - turn + 1 + place, 0)
        goal = jnp.minimum(ix + turn - place, sx - 1)
        leading.append(remote(5 + sy + i, source, through, (first_stop, iy)))
        follows.append(remote(7 + sy + i, through, plane.at[i], (goal, iy), got=i))

    pl.when(to_x & jnp.logical_not(leads | yields))(plane_w.start)

    @pl.when(leads)
    def _():
        for copy in leading:
            copy.start()


    loads[0].wait()
    loads[1].wait()
    for x in range(nx):
        w, a = w_ref[x], a_ref[x]
        for part, value in enumerate((-(w + 0.5 * a), 0.5 * w - a)):
            high, low = split(value)
            mass[part, 0, x * ny : (x + 1) * ny] = high
            mass[part, 1, x * ny : (x + 1) * ny] = low
            for c in range(nz // 128):
                raw[part, c, x : x + 1] = value[ny - 1 : ny, c * 128 : (c + 1) * 128]
    loads[2].wait()
    loads[3].wait()
    for load in loads[4:]:
        load.start()

    def halves(left, right):
        both = dot(jnp.concatenate(split(left), axis=0), right)
        return both[: left.shape[0]] + both[left.shape[0] :]

    for part in range(2):
        table = later_ref[144:320, 0:cells]
        rows = dot(table, mass[part, 0]) + dot(table, mass[part, 1])
        three = halves(rows[48:112] + rows[112:176], later_z_ref[1, 0:nz, 0:128])
        two = halves(rows[0:48], later_z_ref[0, 0:nz])
        t3[part] = three[0:32]
        x3_send[part * 16 : part * 16 + 16] = three[32:48]
        x2_send[part * 32 : part * 32 + 32] = two[0:32]
        for e in range(2):
            row_send[64 + e * 16 + part * 8 : 64 + e * 16 + part * 8 + 8] = two[32:40, e * 128 : e * 128 + 128]
            corner_send[8 + e * 8 + part * 4 : 8 + e * 8 + part * 4 + 4] = two[40:44, e * 128 : e * 128 + 128]
        row_send[96 + part * 4 : 96 + part * 4 + 4] = three[48:52]
        corner_send[24 + part * 4 : 24 + part * 4 + 4] = three[52:56]
        for c in range(nz // 128):
            row_send[part * 32 + c * 8 : part * 32 + c * 8 + 8] = raw[part, c]
            corner_send[part * 4 + c : part * 4 + c + 1] = raw[part, c, nx - 1 : nx]

    pl.when(to_x)(x3.start)
    pl.when(to_xy)(corner.start)
    pl.when(to_y & jnp.logical_not(leads))(row.start)

    pl.when(to_x & jnp.logical_not(leads | yields))(plane_a.start)
    pl.when(to_x)(x2.start)
    pl.when(to_y & leads)(row.start)

    for part in range(2):
        table = later_ref[0:144, 0:cells]
        rows = dot(table, mass[part, 0]) + dot(table, mass[part, 1])
        t2[part] = halves(rows, later_z_ref[0, 0:nz])

    loads[4].wait()
    loads[5].wait()

    def own_level_one(i, carry):
        part, a = i // 3, lax.rem(i, 3)
        table = z_ref[a]
        both = dot(mass[part].reshape(2 * cells, nz), table[0:nz])
        high, low = split(both[0:cells] + both[cells:])
        grid = jnp.where(part == 0, table[nz : nz + 16], jnp.zeros((16, nz // 2), BF16))
        rest = jnp.concatenate([jnp.zeros((2 * HALO, nz // 2), BF16), grid, jnp.zeros((16, nz // 2), BF16)], axis=0)
        for ax in range(3):
            rows = first_ref[ax * 192 : ax * 192 + 192]
            out = dot(rows[:, 0:cells], high) + dot(rows[:, 0:cells], low) + dot(rows[:, cells:], rest)
            one_ref[part, ax, :, a] = out.reshape(3, nx // 2, ny // 2, nz // 2)
        return carry

    lax.fori_loop(0, 6, own_level_one, 0)

    @pl.when(yields)
    def _():
        plane_w.start()
        plane_a.start()

    pl.when(from_y)(row.wait_recv)
    for part in range(2):
        rows = jnp.concatenate([row_got[part * 32 + c * 8 : part * 32 + c * 8 + 8] for c in range(nz // 128)], axis=1)
        edge[part] = jnp.concatenate([rows, jnp.zeros((8, nz), F32)], axis=0)
    high, low = split(edge[...].reshape(32, nz))
    both = jnp.concatenate([high, low], axis=0)
    gap = jnp.zeros((32, nz // 2), BF16)
    table = first_ref[:, cells:].reshape(3, 3, nx // 2, ny // 2, 128)
    head_ref[...] = table[0:2, :, 0].reshape(-1, 128)
    for a in range(3):
        z = dot(both, z_ref[a, 0:nz])
        zh, zl = split(z[0:32] + z[32:64])
        for part in range(2):
            own = slice(part * 16, part * 16 + 16)
            rest = jnp.concatenate([gap, zh[own], gap, zl[own], gap], axis=0)
            add = dot(table[2, 0:2].reshape(-1, 128), rest).reshape(2, nx // 2, ny // 2, nz // 2)
            one_ref[part, 2, 0:2, a, :, 0:8] += add[:, :, 0:8]
            add = dot(table[0:2, 0:2, 1:].reshape(-1, 128), rest).reshape(2, 2, nx // 2 - 1, ny // 2, nz // 2)
            one_ref[part, 0:2, 0:2, a, 1:, 0:8] += add[:, :, :, 0:8]

    pl.when(from_xy)(corner.wait_recv)
    pl.when(from_x)(x3.wait_recv)
    for part in range(2):
        k3[part, 0:16] = x3_got[part * 16 : part * 16 + 16]
        k3[part, 16:20] = row_got[96 + part * 4 : 96 + part * 4 + 4]
        k3[part, 20:24] = corner_got[24 + part * 4 : 24 + part * 4 + 4]
        k3[part, 24:32] = jnp.zeros((8, 128), F32)
        high, low = split(k3[part])
        grid = later_z_ref[1, nz : nz + 16, 0:128]
        if part == 1:
            grid = jnp.zeros_like(grid)
        rest = jnp.concatenate([high, low, grid, jnp.zeros((48, 128), BF16)], axis=0)
        own = t3[part] + dot(later_ref[192:224, cells:], rest)
        blocks[iy, part * 24 : part * 24 + 24] = own[0:24]
    for copy in gathers:
        copy.start()

    for part in range(2):
        edge[part, 8:9] = jnp.concatenate([corner_got[part * 4 + c : part * 4 + c + 1] for c in range(nz // 128)], axis=1)

    for part in range(2):
        k2[part, 0:32] = jnp.zeros((32, nz // 2), F32)
        for e in range(2):
            lanes = slice(e * 128, e * 128 + 128)
            k2[part, 32:40, lanes] = row_got[64 + e * 16 + part * 8 : 64 + e * 16 + part * 8 + 8]
            k2[part, 40:44, lanes] = corner_got[8 + e * 8 + part * 4 : 8 + e * 8 + part * 4 + 4]
        k2[part, 44:48] = jnp.zeros((4, nz // 2), F32)
        high, low = split(k2[part])
        grid = later_z_ref[0, nz : nz + 16]
        if part == 1:
            grid = jnp.zeros_like(grid)
        rest = jnp.concatenate([high, low, grid, jnp.zeros((16, nz // 2), BF16)], axis=0)
        t2_ref[part] = t2[part] + dot(later_ref[0:144, cells:], rest)

    for i in range(2):

        @pl.when(helps[i])
        def _(i=i):
            leading[i].wait_recv()
            follows[i].start()

    @pl.when(from_x)
    def _():
        plane_w.wait_recv()
        plane_a.wait_recv()
        x2.wait_recv()

    loads[6].wait()
    for copy in gathers:
        copy.wait_recv()
    for copy in gathers:
        copy.wait_send()
    pl.when(to_y)(row.wait_send)
    pl.when(to_xy)(corner.wait_send)


    @pl.when(to_x & jnp.logical_not(leads))
    def _():
        plane_w.wait_send()
        plane_a.wait_send()

    @pl.when(leads)
    def _():
        for copy in leading:
            copy.wait_send()

    for i in range(2):
        pl.when(helps[i])(follows[i].wait_send)

    @pl.when(to_x)
    def _():
        x3.wait_send()
        x2.wait_send()


def result_kernel(
    one_ref, t2_ref, x2_ref, blocks, plane, edge, z_ref, head_ref, gather_ref,
    one_hbm, two_hbm, three_hbm, first, two, three, sem,
):
    nz = plane.shape[2]
    count = one_ref.shape[4]
    copies = [pltpu.make_async_copy(one_ref.at[part, 2], one_hbm.at[part, 2], sem.at[part]) for part in range(2)]
    rest = pl.ds(1, count - 1)
    for part in range(2):
        for a in range(2):
            slot = sem.at[2 + 2 * part + a]
            copies.append(
                pltpu.make_async_copy(one_ref.at[part, a, :, :, rest], one_hbm.at[part, a, :, :, rest], slot)
            )
    for copy in copies:
        copy.start()

    _, _, _, _, m, n, depth = two.shape
    for part in range(2):
        whole = t2_ref[part].reshape(3, 3, m, n, 2 * depth)
        for a in range(3):
            for b in range(3):
                for x in range(m):
                    value = whole[a, b, x]
                    if x == 0 and a < 2:
                        base = part * 32 + a * 2 * n
                        if b > 0:
                            value = value + x2_ref[base + (b - 1) * n : base + b * n]
                        else:
                            above = pltpu.roll(x2_ref[base + n : base + 2 * n], 1, 0)
                            line = lax.broadcasted_iota(jnp.int32, above.shape, 0)
                            value = value + jnp.where(line == 0, 0.0, above)
                    two[part, a, b, 1, x] = value[:, 0:depth]
                    two[part, a, b, 2, x] = value[:, depth:]
                    two[part, a, b, 0, x] = pltpu.roll(value[:, depth:], 1, 1)
    copies.append(pltpu.make_async_copy(two, two_hbm, sem.at[10]))
    copies[-1].start()

    shape = three.shape[1:3] + three.shape[4:]
    for part in range(2):
        rows = jnp.concatenate([blocks[g, part * 24 : part * 24 + 24] for g in range(blocks.shape[0])], axis=0)
        high, low = split(rows)
        out = dot(gather_ref[...], jnp.concatenate([high, low], axis=0))
        lane = lax.broadcasted_iota(jnp.int32, out.shape, 1)
        upper = pltpu.roll(out, 64, 1)
        lower = jnp.where(lane == 0, 0.0, pltpu.roll(out, 65, 1))
        three[part, :, :, 1] = out[:, 0:64].reshape(shape)
        three[part, :, :, 2] = upper[:, 0:64].reshape(shape)
        three[part, :, :, 0] = lower[:, 0:64].reshape(shape)
    copies.append(pltpu.make_async_copy(three, three_hbm, sem.at[11]))
    copies[-1].start()
    w, a = plane[0], plane[1]
    value = jnp.concatenate([-(w + 0.5 * a), edge[0], 0.5 * w - a, edge[1]], axis=0)
    high, low = split(value)
    both = jnp.concatenate([high, low], axis=0)
    half = 2 * HALO
    for a in range(3):
        z = dot(both, z_ref[a, 0:nz])
        zh, zl = split(z[0:half] + z[half:])
        for part in range(2):
            own = slice(part * HALO, part * HALO + HALO)
            rest = jnp.concatenate([zh[own], zl[own], jnp.zeros((32, nz // 2), BF16)], axis=0)
            add = dot(head_ref[...], rest)
            first[part, :, :, a] = one_ref[part, 0:2, :, a, 0] + add.reshape(2, 3, -1, nz // 2)
    for part in range(2):
        for a in range(2):
            slot = sem.at[6 + 2 * part + a]
            copy = pltpu.make_async_copy(first.at[part, a], one_hbm.at[part, a, :, :, 0], slot)
            copy.start()
            copies.append(copy)

    for copy in copies:
        copy.wait()


def solution(mesh):
    sx, sy = mesh.shape["gx"], mesh.shape["gy"]

    def local(wave_sq, absorb):
        nx, ny, nz = wave_sq.shape
        first, later = xy_tables(nx, ny, sx, sy)
        tables = [
            jnp.asarray(t.astype(ml_dtypes.bfloat16)) for t in (first, later, z_tables(nz), gather_table(sy, ny // 8))
        ]
        first, later, depth, gather = tables
        half = nz // 2
        level_one = jax.ShapeDtypeStruct((2, 3, 3, 3, nx // 2, ny // 2, nz // 2), F32)
        level_two = jax.ShapeDtypeStruct((2, 3, 3, 3, nx // 4, ny // 4, nz // 4), F32)
        level_three = jax.ShapeDtypeStruct((2, 3, 3, 3, nx // 8, sy * ny // 8, nz // 8), F32)
        parts = pl.pallas_call(
            functools.partial(halo_kernel, sx, sy),
            out_shape=(
                level_one,
                jax.ShapeDtypeStruct((2, 144, half), F32),
                jax.ShapeDtypeStruct((64, half), F32),
                jax.ShapeDtypeStruct((sy, 48, 128), F32),
                jax.ShapeDtypeStruct((2, ny, nz), F32),
                jax.ShapeDtypeStruct((2, 16, nz), F32),
                jax.ShapeDtypeStruct((3, *depth.shape[1:]), BF16),
                jax.ShapeDtypeStruct((3 * ny, 128), BF16),
                jax.ShapeDtypeStruct(gather.shape, BF16),
            ),
            in_specs=[pl.BlockSpec(memory_space=pltpu.HBM)] * 6,
            out_specs=[pl.BlockSpec(memory_space=pltpu.VMEM)] * 9,
            scratch_shapes=[
                pltpu.VMEM((nx, ny, nz), F32),
                pltpu.VMEM((nx, ny, nz), F32),
                pltpu.VMEM(first.shape[1:], BF16),
                pltpu.VMEM(later.shape[1:], BF16),
                pltpu.VMEM((2, *depth.shape[1:]), BF16),
                pltpu.VMEM((2, 2, nx * ny, nz), BF16),
                pltpu.VMEM((104, 128), F32),
                pltpu.VMEM((104, 128), F32),
                pltpu.VMEM((32, 128), F32),
                pltpu.VMEM((32, 128), F32),
                pltpu.VMEM((64, half), F32),
                pltpu.VMEM((32, 128), F32),
                pltpu.VMEM((32, 128), F32),
                pltpu.VMEM((2, 144, half), F32),
                pltpu.VMEM((2, 32, 128), F32),
                pltpu.VMEM((2, HALO, half), F32),
                pltpu.VMEM((2, 32, 128), F32),
                pltpu.VMEM((2, nz // 128, nx, 128), F32),
                pltpu.VMEM((ny, nz), F32),
                pltpu.SemaphoreType.DMA((7,)),
                pltpu.SemaphoreType.DMA((9 + sy,)),
                pltpu.SemaphoreType.DMA((9 + sy,)),
            ],
            compiler_params=pltpu.CompilerParams(
                collective_id=0, has_side_effects=True, vmem_limit_bytes=32 * 1024 * 1024
            ),
        )(*[pltpu.with_memory_space_constraint(v, pltpu.HBM) for v in (wave_sq, absorb, first, later, depth, gather)])
        return pl.pallas_call(
            result_kernel,
            out_shape=(level_one, level_two, level_three),
            in_specs=[pl.BlockSpec(memory_space=pltpu.VMEM)] * 9,
            out_specs=[pl.BlockSpec(memory_space=pltpu.HBM)] * 3,
            scratch_shapes=[
                pltpu.VMEM((2, 2, 3, 3, ny // 2, half), F32),
                pltpu.VMEM(level_two.shape, F32),
                pltpu.VMEM(level_three.shape, F32),
                pltpu.SemaphoreType.DMA((12,)),
            ],
            compiler_params=pltpu.CompilerParams(vmem_limit_bytes=16 * 1024 * 1024),
        )(*parts)

    return jax.shard_map(
        local,
        mesh=mesh,
        in_specs=(P("gx", "gy", None), P("gx", "gy", None)),
        out_specs=(
            P(None, None, None, None, "gx", "gy", None),
            P(None, None, None, None, "gx", "gy", None),
            P(None, None, None, None, "gx", None, None),
        ),
        check_vma=False,
    )
```

```python
import functools

import jax
import jax.numpy as jnp
import ml_dtypes
import numpy as np
from jax import lax
from jax.experimental import pallas as pl
from jax.experimental.pallas import tpu as pltpu
from jax.sharding import PartitionSpec as P

MESH = pl.DeviceIdType.MESH
BF16 = jnp.bfloat16
F32 = jnp.float32
FIRST, MIDDLE, LAST = 0, 1, 2


def hat(distance, width):
    return np.maximum(0.0, 1.0 - np.abs(distance) / width)


def line_weights(cells, level, place):
    width = 2**level
    coarse = cells // width
    fine = np.arange(cells)[None, :]
    node = width * np.arange(coarse)[:, None]
    table = np.stack([hat(fine - node, width) * hat(fine - node - a * width, width) for a in (-1, 0, 1)])
    table /= width
    if place == LAST:
        table[2, -1] = 0.0
    return table


def tail_weights(cells, level, place):
    width = 2**level
    distance = np.arange(cells) - cells
    table = np.stack([hat(distance, width) * hat(distance + width, width), hat(distance, width) ** 2]) / width
    return table * (place != LAST)


def grid_tables(cells):
    lap = np.zeros((cells, 3))
    lap[:] = (-1.0, 2.0, -1.0)
    lap[0, 0] = lap[-1, 2] = 0.0
    one = np.zeros((cells, 3))
    one[:, 1] = 1.0

    def coarsen(band):
        coarse = band.shape[0] // 2
        out = np.zeros((coarse, 3))
        for row in range(coarse):
            for a in (-1, 0, 1):
                if not 0 <= row + a < coarse:
                    continue
                for step, weight in ((-1, 0.25), (0, 0.5), (1, 0.25)):
                    fine = 2 * row + step
                    if fine < 0:
                        continue
                    for b in (-1, 0, 1):
                        distance = abs(fine + b - 2 * (row + a))
                        spread = 1.0 if distance == 0 else 0.5 if distance == 1 else 0.0
                        out[row, a + 1] += weight * spread * band[fine, b + 1]
        return out

    tables = []
    for _ in range(3):
        lap, one = coarsen(lap), coarsen(one)
        tables.append((lap.T, one.T))
    return tables


def two_terms(table):
    high = table.astype(ml_dtypes.bfloat16).astype(np.float64)
    return high, table - high


def row_features(lap, one):
    (lh, ll), (oh, ol) = two_terms(lap), two_terms(one)
    columns = [lh, lh, ll, ll, oh, oh, ol, ol]
    return np.stack(columns + [np.zeros_like(lh)] * 8, axis=1)


def column_features(lap, one):
    (lh, ll), (oh, ol) = two_terms(lap), two_terms(one)
    rows = [oh, ol, oh, ol, lh, ll, lh, ll]
    return np.stack(rows + [np.zeros_like(lh)] * 8, axis=0)


def place_slice(table, place, cells):
    whole = table.shape[1]
    start = {FIRST: 0, MIDDLE: cells, LAST: whole - cells}[place]
    return table[:, start : start + cells]


def grid_rows(grid_x, grid_y, place_x, place_y, cells_x, cells_y):
    lap_x, one_x = (place_slice(t, place_x, cells_x)[:, None, :, None] for t in grid_x)
    lap_y, one_y = (place_slice(t, place_y, cells_y)[None, :, None, :] for t in grid_y)
    lap = (lap_x * one_y + one_x * lap_y).reshape(-1)
    one = (one_x * one_y).reshape(-1)
    return row_features(lap, one)


def padded(rows, count, width=None):
    out = np.zeros((count, rows.shape[1] if width is None else width))
    out[: rows.shape[0], : rows.shape[1]] = rows
    return out


def pair(left, right):
    both = np.einsum("aJi,bKj->abJKij", left, right)
    return both.reshape(-1, left.shape[2] * right.shape[2])


def xy_tables(nx, ny, sx, sy):
    grid_x, grid_y = grid_tables(nx * sx), grid_tables(ny * sy)
    first, later = [], []
    for px in (FIRST, MIDDLE, LAST):
        for py in (FIRST, MIDDLE, LAST):
            wx = [line_weights(nx, k, px) for k in (1, 2, 3)]
            wy = [line_weights(ny, k, py) for k in (1, 2, 3)]
            tx = [tail_weights(nx, k, px)[:, None, :] for k in (1, 2, 3)]
            ty = [tail_weights(ny, k, py)[:, None, :] for k in (1, 2, 3)]

            own = pair(wx[0], wy[0])
            head_x = np.zeros((3, nx // 2, 1))
            head_x[0:2, 0, 0] = 0.125 * (px != FIRST)
            head_y = np.zeros((3, ny // 2, 1))
            head_y[0:2, 0, 0] = 0.125 * (py != FIRST)
            halo = np.concatenate([pair(head_x, wy[0]), pair(wx[0], head_y), pair(head_x, head_y)], axis=1)
            halo = padded(halo, halo.shape[0], HALO)
            grid = grid_rows(grid_x[0], grid_y[0], px, py, nx // 2, ny // 2)
            first.append(padded(np.concatenate([own, halo, halo, grid], axis=1), own.shape[0], nx * ny + 128))

            m, n = nx // 4, ny // 4
            own = pair(wx[1], wy[1])
            send = [pair(tx[1], wy[1][1:]), pair(wx[1][1:], ty[1]), pair(tx[1], ty[1])]
            rows2 = padded(np.concatenate([own, *send]), 192)
            take = np.zeros((3, 3, m, n, HALO))
            for a in range(2):
                for j in range(n):
                    take[a, 1, 0, j, a * 2 * n + j] = 1.0
                    take[a, 2, 0, j, a * 2 * n + n + j] = 1.0
                    if j + 1 < n:
                        take[a, 0, 0, j + 1, a * 2 * n + n + j] = 1.0
                for i in range(m):
                    own_e, own_f = 4 * n + a * m + i, 4 * n + (2 + a) * m + i
                    take[1, a, i, 0, own_e] = 1.0
                    take[2, a, i, 0, own_f] = 1.0
                    if i + 1 < m:
                        take[0, a, i + 1, 0, own_f] = 1.0
                for b in range(2):
                    take[a, b, 0, 0, 4 * n + 4 * m + 2 * a + b] = 1.0
            take = take.reshape(-1, HALO)
            grid = grid_rows(grid_x[1], grid_y[1], px, py, m, n)
            take2 = np.concatenate([take, take, grid], axis=1)

            n = ny // 8
            own = padded(pair(wx[2], wy[2][1:]), 32)
            send = [pair(tx[2], wy[2][1:]), pair(wx[2][1:], ty[2]), pair(tx[2], ty[2])]
            rows3 = padded(np.concatenate([own, *send]), 64)
            take = np.zeros((3, 2, n, 32))
            for a in range(2):
                for e in range(2):
                    for j in range(n):
                        take[a, e, j, (a * 2 + e) * n + j] = 1.0
                take[1 + a, 0, 0, 4 * n + 2 * a + 1] = 1.0
                take[a, 0, 0, 4 * n + 4 + 2 * a + 1] = 1.0
            take = take.reshape(-1, 32)
            grid = grid_rows(grid_x[2], grid_y[2], px, py, 1, n).reshape(3, 3, n, 16)[:, 1:].reshape(-1, 16)
            take3 = np.concatenate([take, take, grid], axis=1)

            table = np.zeros((320, nx * ny + 128))
            high, low = two_terms(rows3)
            table[:, : nx * ny] = np.concatenate([rows2, high, low])
            table[: take2.shape[0], nx * ny : nx * ny + take2.shape[1]] = take2
            table[192 : 192 + take3.shape[0], nx * ny : nx * ny + take3.shape[1]] = take3
            later.append(table)
    return np.stack(first), np.stack(later)


def z_tables(nz):
    grid = grid_tables(nz)
    half = nz // 2
    blocks = []
    one = line_weights(nz, 1, LAST)
    one[0, 0] = 0.0
    for a in range(3):
        blocks.append(np.concatenate([one[a].T, column_features(grid[0][0][a], grid[0][1][a])]))
    for k in (2, 3):
        table = line_weights(nz, k, LAST)
        columns = [
            np.concatenate([table[a].T, column_features(grid[k - 1][0][a], grid[k - 1][1][a])]) for a in (1, 2)
        ]
        block = np.concatenate(columns, axis=1)
        blocks.append(padded(block, nz + 16, half))
    return np.stack(blocks)


def gather_table(parts, n):
    table = np.zeros((3, 3, parts * n, parts, 3, 2, n))
    for a in range(3):
        for g in range(parts):
            for j in range(n):
                row = g * n + j
                table[a, 1, row, g, a, 0, j] = 1.0
                table[a, 2, row, g, a, 1, j] = 1.0
                if row + 1 < parts * n:
                    table[a, 0, row + 1, g, a, 1, j] = 1.0
    table = table.reshape(9 * parts * n, -1)
    return np.concatenate([table, table], axis=1)


HALO = 48
TURNS = 4
RELAYS = (7, 3)


def split(value):
    high = value.astype(BF16)
    return high, (value - high.astype(F32)).astype(BF16)


def dot(left, right):
    return jnp.dot(left, right, preferred_element_type=F32)


def exact_dot(left, value):
    high, low = split(value)
    return dot(left, high) + dot(left, low)


def halo_kernel(
    sx, sy,
    w_hbm, a_hbm, first_hbm, later_hbm, z_hbm, gather_hbm,
    one_ref, t2_ref, x2_got, blocks, plane, edge, z_ref, head_ref, gather_ref,
    w_ref, a_ref, first_ref, later_ref, later_z_ref,
    mass, row_send, row_got, corner_send, corner_got,
    x2_send, x3_send, x3_got, t2, t3, k2, k3, raw, through,
    load_sem, send_sem, got_sem,
):
    ix, iy = lax.axis_index("gx"), lax.axis_index("gy")
    nx, ny, nz = w_hbm.shape
    cells = nx * ny
    next_x, last_x = lax.rem(ix + 1, sx), lax.rem(ix + sx - 1, sx)
    next_y, last_y = lax.rem(iy + 1, sy), lax.rem(iy + sy - 1, sy)
    from_x, to_x, from_y, to_y = ix > 0, ix < sx - 1, iy > 0, iy < sy - 1
    from_xy, to_xy = from_x & from_y, to_x & to_y
    turn = sx // TURNS
    turning = sx == TURNS * 32
    at = lax.rem(ix, turn)
    leads = to_x & (at == turn - 1) & turning
    helps = [(ix < sx - turn) & (at == place) & turning for place in RELAYS]
    waits = from_x & (at == 0) & turning
    upper = iy >= sy // 2
    yields = to_x & turning & (((at == turn - 2) & upper) | ((at == turn - 4) & jnp.logical_not(upper)))
    peers = [lax.rem(iy + step, sy) for step in range(1, sy)]

    place_x = jnp.where(ix == 0, FIRST, jnp.where(ix == sx - 1, LAST, MIDDLE))
    place_y = jnp.where(iy == 0, FIRST, jnp.where(iy == sy - 1, LAST, MIDDLE))
    place = place_x * 3 + place_y
    loads = [
        pltpu.make_async_copy(src, dst, load_sem.at[i])
        for i, (src, dst) in enumerate(
            (
                (w_hbm, w_ref),
                (a_hbm, a_ref),
                (later_hbm.at[place], later_ref),
                (z_hbm.at[pl.ds(3, 2)], later_z_ref),
                (z_hbm.at[pl.ds(0, 3)], z_ref),
                (first_hbm.at[place], first_ref),
                (gather_hbm, gather_ref),
            )
        )
    ]
    for load in loads[:4]:
        load.start()

    @pl.when(jnp.logical_not(from_x))
    def _():
        plane[...] = jnp.zeros_like(plane)
        x2_got[...] = jnp.zeros_like(x2_got)
        x3_got[...] = jnp.zeros_like(x3_got)

    @pl.when(jnp.logical_not(from_y))
    def _():
        row_got[...] = jnp.zeros_like(row_got)

    @pl.when(jnp.logical_not(from_xy))
    def _():
        corner_got[...] = jnp.zeros_like(corner_got)

    def signal(*device):
        pl.semaphore_signal(barrier, inc=1, device_id=device, device_id_type=MESH)

    barrier = pltpu.get_barrier_semaphore()
    for p in peers:
        signal(ix, p)
    pl.when(from_x)(lambda: signal(last_x, iy))
    pl.when(from_xy)(lambda: signal(last_x, last_y))
    for i, place in enumerate(RELAYS):
        pl.when(waits)(lambda place=place: signal(ix - turn + place, iy))
        pl.when(helps[i])(lambda place=place: signal(ix + turn - 1 - place, iy))
    sends_to = [flag.astype(jnp.int32) for flag in (to_x, to_xy, leads, leads, *helps)]
    pl.semaphore_wait(barrier, sy - 1 + sum(sends_to))

    def remote(slot, src, dst, device, got=None):
        got = slot if got is None else got
        return pltpu.make_async_remote_copy(
            src_ref=src, dst_ref=dst, send_sem=send_sem.at[slot], recv_sem=got_sem.at[got],
            device_id=device, device_id_type=MESH,
        )

    plane_w = remote(0, w_hbm.at[nx - 1], plane.at[0], (next_x, iy))
    plane_a = remote(1, a_hbm.at[nx - 1], plane.at[1], (next_x, iy))
    x3 = remote(2, x3_send, x3_got, (next_x, iy))
    x2 = remote(3, x2_send, x2_got, (next_x, iy))
    row = remote(4, row_send, row_got, (ix, next_y))
    corner = remote(5, corner_send, corner_got, (next_x, next_y))
    gathers = [remote(6 + i, blocks.at[iy], blocks.at[iy], (ix, p)) for i, p in enumerate(peers)]

    leading, follows = [], []
    for i, place in enumerate(RELAYS):
        source = (w_hbm, a_hbm)[i].at[nx - 1]
        first_stop = jnp.maximum(ix - turn + 1 + place, 0)
        goal = jnp.minimum(ix + turn - place, sx - 1)
        leading.append(remote(5 + sy + i, source, through, (first_stop, iy)))
        follows.append(remote(7 + sy + i, through, plane.at[i], (goal, iy), got=i))

    pl.when(to_x & jnp.logical_not(leads | yields))(plane_w.start)

    @pl.when(leads)
    def _():
        for copy in leading:
            copy.start()


    loads[0].wait()
    loads[1].wait()
    for x in range(nx):
        w, a = w_ref[x], a_ref[x]
        for part, value in enumerate((-(w + 0.5 * a), 0.5 * w - a)):
            high, low = split(value)
            mass[part, 0, x * ny : (x + 1) * ny] = high
            mass[part, 1, x * ny : (x + 1) * ny] = low
            for c in range(nz // 128):
                raw[part, c, x : x + 1] = value[ny - 1 : ny, c * 128 : (c + 1) * 128]
    loads[2].wait()
    loads[3].wait()
    for load in loads[4:]:
        load.start()

    def halves(left, right):
        both = dot(jnp.concatenate(split(left), axis=0), right)
        return both[: left.shape[0]] + both[left.shape[0] :]

    for part in range(2):
        table = later_ref[144:320, 0:cells]
        rows = dot(table, mass[part, 0]) + dot(table, mass[part, 1])
        three = halves(rows[48:112] + rows[112:176], later_z_ref[1, 0:nz, 0:128])
        two = halves(rows[0:48], later_z_ref[0, 0:nz])
        t3[part] = three[0:32]
        x3_send[part * 16 : part * 16 + 16] = three[32:48]
        x2_send[part * 32 : part * 32 + 32] = two[0:32]
        for e in range(2):
            row_send[64 + e * 16 + part * 8 : 64 + e * 16 + part * 8 + 8] = two[32:40, e * 128 : e * 128 + 128]
            corner_send[8 + e * 8 + part * 4 : 8 + e * 8 + part * 4 + 4] = two[40:44, e * 128 : e * 128 + 128]
        row_send[96 + part * 4 : 96 + part * 4 + 4] = three[48:52]
        corner_send[24 + part * 4 : 24 + part * 4 + 4] = three[52:56]
        for c in range(nz // 128):
            row_send[part * 32 + c * 8 : part * 32 + c * 8 + 8] = raw[part, c]
            corner_send[part * 4 + c : part * 4 + c + 1] = raw[part, c, nx - 1 : nx]

    pl.when(to_x)(x3.start)
    pl.when(to_xy)(corner.start)
    pl.when(to_y & jnp.logical_not(leads))(row.start)

    pl.when(to_x & jnp.logical_not(leads | yields))(plane_a.start)
    pl.when(to_x & jnp.logical_not(yields))(x2.start)
    pl.when(to_y & leads)(row.start)

    for part in range(2):
        table = later_ref[0:144, 0:cells]
        rows = dot(table, mass[part, 0]) + dot(table, mass[part, 1])
        t2[part] = halves(rows, later_z_ref[0, 0:nz])

    loads[4].wait()
    loads[5].wait()

    def own_level_one(i, carry):
        part, a = i // 3, lax.rem(i, 3)
        table = z_ref[a]
        both = dot(mass[part].reshape(2 * cells, nz), table[0:nz])
        high, low = split(both[0:cells] + both[cells:])
        grid = jnp.where(part == 0, table[nz : nz + 16], jnp.zeros((16, nz // 2), BF16))
        rest = jnp.concatenate([jnp.zeros((2 * HALO, nz // 2), BF16), grid, jnp.zeros((16, nz // 2), BF16)], axis=0)
        for ax in range(3):
            rows = first_ref[ax * 192 : ax * 192 + 192]
            out = dot(rows[:, 0:cells], high) + dot(rows[:, 0:cells], low) + dot(rows[:, cells:], rest)
            one_ref[part, ax, :, a] = out.reshape(3, nx // 2, ny // 2, nz // 2)
        return carry

    lax.fori_loop(0, 6, own_level_one, 0)

    @pl.when(yields)
    def _():
        x2.start()
        plane_w.start()
        plane_a.start()

    pl.when(from_y)(row.wait_recv)
    for part in range(2):
        rows = jnp.concatenate([row_got[part * 32 + c * 8 : part * 32 + c * 8 + 8] for c in range(nz // 128)], axis=1)
        edge[part] = jnp.concatenate([rows, jnp.zeros((8, nz), F32)], axis=0)
    high, low = split(edge[...].reshape(32, nz))
    both = jnp.concatenate([high, low], axis=0)
    gap = jnp.zeros((32, nz // 2), BF16)
    table = first_ref[:, cells:].reshape(3, 3, nx // 2, ny // 2, 128)
    head_ref[...] = table[0:2, :, 0].reshape(-1, 128)
    for a in range(3):
        z = dot(both, z_ref[a, 0:nz])
        zh, zl = split(z[0:32] + z[32:64])
        for part in range(2):
            own = slice(part * 16, part * 16 + 16)
            rest = jnp.concatenate([gap, zh[own], gap, zl[own], gap], axis=0)
            add = dot(table[2, 0:2].reshape(-1, 128), rest).reshape(2, nx // 2, ny // 2, nz // 2)
            one_ref[part, 2, 0:2, a, :, 0:8] += add[:, :, 0:8]
            add = dot(table[0:2, 0:2, 1:].reshape(-1, 128), rest).reshape(2, 2, nx // 2 - 1, ny // 2, nz // 2)
            one_ref[part, 0:2, 0:2, a, 1:, 0:8] += add[:, :, :, 0:8]

    pl.when(from_xy)(corner.wait_recv)
    pl.when(from_x)(x3.wait_recv)
    for part in range(2):
        k3[part, 0:16] = x3_got[part * 16 : part * 16 + 16]
        k3[part, 16:20] = row_got[96 + part * 4 : 96 + part * 4 + 4]
        k3[part, 20:24] = corner_got[24 + part * 4 : 24 + part * 4 + 4]
        k3[part, 24:32] = jnp.zeros((8, 128), F32)
        high, low = split(k3[part])
        grid = later_z_ref[1, nz : nz + 16, 0:128]
        if part == 1:
            grid = jnp.zeros_like(grid)
        rest = jnp.concatenate([high, low, grid, jnp.zeros((48, 128), BF16)], axis=0)
        own = t3[part] + dot(later_ref[192:224, cells:], rest)
        blocks[iy, part * 24 : part * 24 + 24] = own[0:24]
    for copy in gathers:
        copy.start()

    for part in range(2):
        edge[part, 8:9] = jnp.concatenate([corner_got[part * 4 + c : part * 4 + c + 1] for c in range(nz // 128)], axis=1)

    for part in range(2):
        k2[part, 0:32] = jnp.zeros((32, nz // 2), F32)
        for e in range(2):
            lanes = slice(e * 128, e * 128 + 128)
            k2[part, 32:40, lanes] = row_got[64 + e * 16 + part * 8 : 64 + e * 16 + part * 8 + 8]
            k2[part, 40:44, lanes] = corner_got[8 + e * 8 + part * 4 : 8 + e * 8 + part * 4 + 4]
        k2[part, 44:48] = jnp.zeros((4, nz // 2), F32)
        high, low = split(k2[part])
        grid = later_z_ref[0, nz : nz + 16]
        if part == 1:
            grid = jnp.zeros_like(grid)
        rest = jnp.concatenate([high, low, grid, jnp.zeros((16, nz // 2), BF16)], axis=0)
        t2_ref[part] = t2[part] + dot(later_ref[0:144, cells:], rest)

    for i in range(2):

        @pl.when(helps[i])
        def _(i=i):
            leading[i].wait_recv()
            follows[i].start()

    @pl.when(from_x)
    def _():
        plane_w.wait_recv()
        plane_a.wait_recv()
        x2.wait_recv()

    loads[6].wait()
    for copy in gathers:
        copy.wait_recv()
    for copy in gathers:
        copy.wait_send()
    pl.when(to_y)(row.wait_send)
    pl.when(to_xy)(corner.wait_send)


    @pl.when(to_x & jnp.logical_not(leads))
    def _():
        plane_w.wait_send()
        plane_a.wait_send()

    @pl.when(leads)
    def _():
        for copy in leading:
            copy.wait_send()

    for i in range(2):
        pl.when(helps[i])(follows[i].wait_send)

    @pl.when(to_x)
    def _():
        x3.wait_send()
        x2.wait_send()


def result_kernel(
    one_ref, t2_ref, x2_ref, blocks, plane, edge, z_ref, head_ref, gather_ref,
    one_hbm, two_hbm, three_hbm, first, two, three, sem,
):
    nz = plane.shape[2]
    count = one_ref.shape[4]
    copies = [pltpu.make_async_copy(one_ref.at[part, 2], one_hbm.at[part, 2], sem.at[part]) for part in range(2)]
    rest = pl.ds(1, count - 1)
    for part in range(2):
        for a in range(2):
            slot = sem.at[2 + 2 * part + a]
            copies.append(
                pltpu.make_async_copy(one_ref.at[part, a, :, :, rest], one_hbm.at[part, a, :, :, rest], slot)
            )
    for copy in copies:
        copy.start()

    _, _, _, _, m, n, depth = two.shape
    for part in range(2):
        whole = t2_ref[part].reshape(3, 3, m, n, 2 * depth)
        for a in range(3):
            for b in range(3):
                for x in range(m):
                    value = whole[a, b, x]
                    if x == 0 and a < 2:
                        base = part * 32 + a * 2 * n
                        if b > 0:
                            value = value + x2_ref[base + (b - 1) * n : base + b * n]
                        else:
                            above = pltpu.roll(x2_ref[base + n : base + 2 * n], 1, 0)
                            line = lax.broadcasted_iota(jnp.int32, above.shape, 0)
                            value = value + jnp.where(line == 0, 0.0, above)
                    two[part, a, b, 1, x] = value[:, 0:depth]
                    two[part, a, b, 2, x] = value[:, depth:]
                    two[part, a, b, 0, x] = pltpu.roll(value[:, depth:], 1, 1)
    copies.append(pltpu.make_async_copy(two, two_hbm, sem.at[10]))
    copies[-1].start()

    shape = three.shape[1:3] + three.shape[4:]
    for part in range(2):
        rows = jnp.concatenate([blocks[g, part * 24 : part * 24 + 24] for g in range(blocks.shape[0])], axis=0)
        high, low = split(rows)
        out = dot(gather_ref[...], jnp.concatenate([high, low], axis=0))
        lane = lax.broadcasted_iota(jnp.int32, out.shape, 1)
        upper = pltpu.roll(out, 64, 1)
        lower = jnp.where(lane == 0, 0.0, pltpu.roll(out, 65, 1))
        three[part, :, :, 1] = out[:, 0:64].reshape(shape)
        three[part, :, :, 2] = upper[:, 0:64].reshape(shape)
        three[part, :, :, 0] = lower[:, 0:64].reshape(shape)
    copies.append(pltpu.make_async_copy(three, three_hbm, sem.at[11]))
    copies[-1].start()
    w, a = plane[0], plane[1]
    value = jnp.concatenate([-(w + 0.5 * a), edge[0], 0.5 * w - a, edge[1]], axis=0)
    high, low = split(value)
    both = jnp.concatenate([high, low], axis=0)
    half = 2 * HALO
    for a in range(3):
        z = dot(both, z_ref[a, 0:nz])
        zh, zl = split(z[0:half] + z[half:])
        for part in range(2):
            own = slice(part * HALO, part * HALO + HALO)
            rest = jnp.concatenate([zh[own], zl[own], jnp.zeros((32, nz // 2), BF16)], axis=0)
            add = dot(head_ref[...], rest)
            first[part, :, :, a] = one_ref[part, 0:2, :, a, 0] + add.reshape(2, 3, -1, nz // 2)
    for part in range(2):
        for a in range(2):
            slot = sem.at[6 + 2 * part + a]
            copy = pltpu.make_async_copy(first.at[part, a], one_hbm.at[part, a, :, :, 0], slot)
            copy.start()
            copies.append(copy)

    for copy in copies:
        copy.wait()


def solution(mesh):
    sx, sy = mesh.shape["gx"], mesh.shape["gy"]

    def local(wave_sq, absorb):
        nx, ny, nz = wave_sq.shape
        first, later = xy_tables(nx, ny, sx, sy)
        tables = [
            jnp.asarray(t.astype(ml_dtypes.bfloat16)) for t in (first, later, z_tables(nz), gather_table(sy, ny // 8))
        ]
        first, later, depth, gather = tables
        half = nz // 2
        level_one = jax.ShapeDtypeStruct((2, 3, 3, 3, nx // 2, ny // 2, nz // 2), F32)
        level_two = jax.ShapeDtypeStruct((2, 3, 3, 3, nx // 4, ny // 4, nz // 4), F32)
        level_three = jax.ShapeDtypeStruct((2, 3, 3, 3, nx // 8, sy * ny // 8, nz // 8), F32)
        parts = pl.pallas_call(
            functools.partial(halo_kernel, sx, sy),
            out_shape=(
                level_one,
                jax.ShapeDtypeStruct((2, 144, half), F32),
                jax.ShapeDtypeStruct((64, half), F32),
                jax.ShapeDtypeStruct((sy, 48, 128), F32),
                jax.ShapeDtypeStruct((2, ny, nz), F32),
                jax.ShapeDtypeStruct((2, 16, nz), F32),
                jax.ShapeDtypeStruct((3, *depth.shape[1:]), BF16),
                jax.ShapeDtypeStruct((3 * ny, 128), BF16),
                jax.ShapeDtypeStruct(gather.shape, BF16),
            ),
            in_specs=[pl.BlockSpec(memory_space=pltpu.HBM)] * 6,
            out_specs=[pl.BlockSpec(memory_space=pltpu.VMEM)] * 9,
            scratch_shapes=[
                pltpu.VMEM((nx, ny, nz), F32),
                pltpu.VMEM((nx, ny, nz), F32),
                pltpu.VMEM(first.shape[1:], BF16),
                pltpu.VMEM(later.shape[1:], BF16),
                pltpu.VMEM((2, *depth.shape[1:]), BF16),
                pltpu.VMEM((2, 2, nx * ny, nz), BF16),
                pltpu.VMEM((104, 128), F32),
                pltpu.VMEM((104, 128), F32),
                pltpu.VMEM((32, 128), F32),
                pltpu.VMEM((32, 128), F32),
                pltpu.VMEM((64, half), F32),
                pltpu.VMEM((32, 128), F32),
                pltpu.VMEM((32, 128), F32),
                pltpu.VMEM((2, 144, half), F32),
                pltpu.VMEM((2, 32, 128), F32),
                pltpu.VMEM((2, HALO, half), F32),
                pltpu.VMEM((2, 32, 128), F32),
                pltpu.VMEM((2, nz // 128, nx, 128), F32),
                pltpu.VMEM((ny, nz), F32),
                pltpu.SemaphoreType.DMA((7,)),
                pltpu.SemaphoreType.DMA((9 + sy,)),
                pltpu.SemaphoreType.DMA((9 + sy,)),
            ],
            compiler_params=pltpu.CompilerParams(
                collective_id=0, has_side_effects=True, vmem_limit_bytes=32 * 1024 * 1024
            ),
        )(*[pltpu.with_memory_space_constraint(v, pltpu.HBM) for v in (wave_sq, absorb, first, later, depth, gather)])
        return pl.pallas_call(
            result_kernel,
            out_shape=(level_one, level_two, level_three),
            in_specs=[pl.BlockSpec(memory_space=pltpu.VMEM)] * 9,
            out_specs=[pl.BlockSpec(memory_space=pltpu.HBM)] * 3,
            scratch_shapes=[
                pltpu.VMEM((2, 2, 3, 3, ny // 2, half), F32),
                pltpu.VMEM(level_two.shape, F32),
                pltpu.VMEM(level_three.shape, F32),
                pltpu.SemaphoreType.DMA((12,)),
            ],
            compiler_params=pltpu.CompilerParams(vmem_limit_bytes=16 * 1024 * 1024),
        )(*parts)

    return jax.shard_map(
        local,
        mesh=mesh,
        in_specs=(P("gx", "gy", None), P("gx", "gy", None)),
        out_specs=(
            P(None, None, None, None, "gx", "gy", None),
            P(None, None, None, None, "gx", "gy", None),
            P(None, None, None, None, "gx", None, None),
        ),
        check_vma=False,
    )
```
